256 devices in a mesh: row: 64 (over y, z, core), col: 4 (over x).
Axes of the slice: x: 4, y: 4, z: 8, core: 2. Of those that a mesh axis runs over, the one named last changes fastest.
Arguments:
- entity_feats: bfloat16 [65536, 256], P(('col', 'row')), may hold values from -6 to 6
- class_map: int32 [65536], P(('col', 'row')), may hold values from 0 to 127, as said below
- tile_values: bfloat16 [8192, 128, 128], P(('row', 'col')), may hold values from -0.09375 to 0.09375
- tile_rows: int32 [8192], P(('row', 'col')), may hold values from 0 to 3
- tile_column_index: int32 [8192], P(('row', 'col')), may hold values from 0 to 63
- tile_rels: int32 [8192], P(('row', 'col')), may hold values from 0 to 499
- tile_counts: int32 [256], P(('row', 'col')), may hold values from 4 to 32, as said below
- coefficients: bfloat16 [500, 8], replicated, may hold values from -2 to 2
- bases: bfloat16 [8, 256, 256], replicated, may hold values from -0.375 to 0.375
- cotangent: bfloat16 [32768, 256], P(('row', 'col')), may hold values from -6 to 6
Outputs:
- layer_out: bfloat16 [32768, 256], P(('row', 'col'))
- grad_entities: float32 [65536, 256], P(('col', 'row'))
- grad_bases: float32 [8, 256, 256], replicated
- grad_coef: float32 [500, 8], replicated
The draws below stay inside these ranges and needn't reach their ends.
Inputs may be any that keep to these rules, and one draw needn't show every extreme that they name: `class_map`: within every block of 256 entities, every class number 0 to 127 occurs at least once. `tile_counts`: tile slots of a device from its count onward are unused; some device has all 32 slots live in every draw.
All inputs are finite; a program needn't handle non-finite values.
Results may differ from the reference program's by a relative error of at most 0.006.
Values may be sent and summed in bfloat16 or wider, within the bound.
No kernel may reach another device: no remote copies, remote signals or barrier semaphores. Data moves between devices by JAX's collectives and lax.ppermute only.
A program may use at most 128 MiB of HBM per device.

```python
import math
import jax
import jax.numpy as jnp
import numpy as np
from jax import lax

H = 256
B = 8
R = 500
TILE = 128
NODE_DEV = 128
TILES_PER_DEVICE = 32
ENT_DEV = 256
NODES = 32768
ENTS = 65536
TILES = 8192
TR_DEV = 4
TC_DEV = 64
N_ROW = 64
N_COL = 4


def draw_class_map(key, part):
    blocks = ENTS // ENT_DEV

    def one_block(subkey):
        leading_entry = jax.random.permutation(jax.random.fold_in(subkey, 1), NODE_DEV).astype(jnp.int32)
        rest = jax.random.randint(jax.random.fold_in(subkey, 2), (ENT_DEV - NODE_DEV,), 0, NODE_DEV).astype(jnp.int32)
        joined = jnp.concatenate([leading_entry, rest])
        return jax.random.permutation(jax.random.fold_in(subkey, 3), joined)
    subkeys = jax.random.split(jax.random.fold_in(key, 7), blocks)
    return jax.vmap(one_block)(subkeys).reshape(ENTS).astype(jnp.int32)


def draw_tile_counts(key, part):
    devices = TILES // TILES_PER_DEVICE
    lighter = jax.random.randint(jax.random.fold_in(key, 11), (devices,), TILES_PER_DEVICE // 8, TILES_PER_DEVICE // 2 + 1)
    lucky = jax.random.randint(jax.random.fold_in(key, 12), (devices,), 0, 16) == 0
    chosen = jax.random.randint(jax.random.fold_in(key, 13), (), 0, devices)
    full = lucky | (jnp.arange(devices, dtype=jnp.int32) == chosen)
    return jnp.where(full, TILES_PER_DEVICE, lighter).astype(jnp.int32)


def with_ends(array, stream_key, low, top_value):
    place = [jax.random.randint(jax.random.fold_in(stream_key, axis), (), 0, length) for axis, length in enumerate(array.shape)]
    main_axis = array.shape.index(max(array.shape))
    neighbour = place[:main_axis] + [(place[main_axis] + 1) % array.shape[main_axis]] + place[main_axis + 1:]
    return array.at[tuple(place)].set(low).at[tuple(neighbour)].set(top_value)


def block_scale(key, extent, cuts, low, top_value):
    level = 1.0
    for position, blocks in cuts:
        steps = jax.random.uniform(jax.random.fold_in(jax.random.fold_in(key, 6), position), (blocks,), jnp.float32, low / len(cuts), top_value / len(cuts))
        level = level * jnp.repeat(jnp.exp(steps), extent[position] // blocks).reshape((-1,) + (1,) * (len(extent) - 1 - position))
    return level


def rank_table(count, slope):
    loads = [(1 << 20) // math.isqrt(rank ** slope) + 1 for rank in range(1, count + 1)]
    deviation = 1 + sum(loads) // (1 << 30)
    return np.cumsum(np.array([max(1, weight // deviation) for weight in loads]))


def skewed_ids(stream_key, shape, count, lean):
    grid = rank_table(count, lean)
    ticket = jax.random.randint(jax.random.fold_in(stream_key, 1), shape, 0, int(grid[count - 1]))
    rank = jnp.searchsorted(jnp.asarray(grid, jnp.int32), ticket, side="right")
    return jax.random.permutation(jax.random.fold_in(stream_key, 2), count)[rank].astype(jnp.int32)


def normal_values(key, extent, width, limit, cuts=(), kind=jnp.bfloat16):
    drawn = width * jax.random.normal(key, extent, jnp.float32)
    if cuts:
        drawn = drawn * block_scale(key, extent, cuts, -0.22, 0.18)
    return jnp.clip(drawn, -limit, limit).astype(kind)


def setup_inputs(seed: int = 0) -> dict:
    seeds = jax.random.split(jax.random.key(seed), 11)
    return {
        "entity_feats": normal_values(seeds[0], (ENTS, H), 1.0, 6.0, ((0, 256),)),
        "class_map": draw_class_map(jax.random.fold_in(seeds[10], 71), 0),
        "tile_values": normal_values(seeds[2], (TILES, TILE, TILE), (1.0 / (TILE * TILES_PER_DEVICE) ** 0.5), 0.09375, ((0, 256),)),
        "tile_rows": with_ends(jax.random.randint(seeds[3], (TILES,), 0, TR_DEV), jax.random.fold_in(seeds[3], 1), 0, TR_DEV - 1).astype(jnp.int32),
        "tile_column_index": with_ends(jax.random.randint(seeds[4], (TILES,), 0, TC_DEV), jax.random.fold_in(seeds[4], 1), 0, TC_DEV - 1).astype(jnp.int32),
        "tile_rels": with_ends(skewed_ids(seeds[5], (TILES,), R, 2), jax.random.fold_in(seeds[5], 3), 0, R - 1).astype(jnp.int32),
        "tile_counts": draw_tile_counts(jax.random.fold_in(seeds[10], 71), 0),
        "coefficients": normal_values(seeds[7], (R, B), B ** -0.5, 2.0),
        "bases": normal_values(seeds[8], (B, H, H), H ** -0.5, 0.375),
        "cotangent": normal_values(seeds[9], (NODES, H), 1.0, 6.0, ((0, 256),)),
    }


def reference(entity_feats, class_map, tile_values, tile_rows, tile_column_index, tile_rels, tile_counts, coefficients, bases, cotangent):
    devices = N_ROW * N_COL
    classes = NODE_DEV * devices
    rblock = NODE_DEV * N_COL
    cblock = NODE_DEV * N_ROW
    trows = rblock // TILE
    tile_column_list = cblock // TILE
    blocks = jnp.arange(ENTS, dtype=jnp.int32) // ENT_DEV
    owner = (blocks * NODE_DEV + class_map).astype(jnp.int32)
    sums = jax.ops.segment_sum(entity_feats.astype(jnp.float32), owner, num_segments=classes)
    counts = jax.ops.segment_sum(jnp.ones((ENTS,), jnp.float32), owner, num_segments=classes)
    class_feat = (sums / counts[:, None]).astype(jnp.bfloat16)
    stacked = bases.reshape(B * H, H)
    basis_grads = jnp.dot(cotangent, stacked.T, preferred_element_type=jnp.float32).astype(jnp.bfloat16)

    def per_device(carry, device):
        out_acc, dv_acc, dcoef_acc, dx_acc = carry
        rowidx = device // N_COL
        colidx = device % N_COL
        leading_entry = (device * TILES_PER_DEVICE).astype(jnp.int32)
        values = lax.dynamic_slice_in_dim(tile_values, leading_entry, TILES_PER_DEVICE, 0).astype(jnp.float32)
        trs = lax.dynamic_slice_in_dim(tile_rows, leading_entry, TILES_PER_DEVICE, 0)
        tile_column_slice = lax.dynamic_slice_in_dim(tile_column_index, leading_entry, TILES_PER_DEVICE, 0)
        rels = lax.dynamic_slice_in_dim(tile_rels, leading_entry, TILES_PER_DEVICE, 0)
        live = (jnp.arange(TILES_PER_DEVICE, dtype=jnp.int32) < tile_counts[device]).astype(jnp.float32)
        sender_device = lax.dynamic_slice_in_dim(class_feat, (colidx * cblock).astype(jnp.int32), cblock, 0).reshape(tile_column_list, TILE, H)
        selected_entries = jnp.take(sender_device, tile_column_slice, axis=0).astype(jnp.float32)
        messages = jnp.einsum("kij,kjh->kih", values, selected_entries).astype(jnp.bfloat16)
        coef_k = jnp.take(coefficients, rels, axis=0).astype(jnp.float32) * live[:, None]
        pick_row = (trs[:, None] == jnp.arange(trows, dtype=jnp.int32)[None, :]).astype(jnp.float32)
        weights = pick_row[:, :, None] * coef_k[:, None, :]
        part = jnp.einsum("ktb,kih->tibh", weights, messages.astype(jnp.float32)).astype(jnp.bfloat16).reshape(rblock, B * H)
        out_part = jnp.dot(part, stacked, preferred_element_type=jnp.float32)
        start = (rowidx * rblock).astype(jnp.int32)
        out_acc = lax.dynamic_update_slice_in_dim(out_acc, lax.dynamic_slice_in_dim(out_acc, start, rblock, 0) + out_part, start, 0)
        dout_rows = lax.dynamic_slice_in_dim(cotangent, start, rblock, 0)
        dv_acc = dv_acc + jnp.dot(part.T, dout_rows, preferred_element_type=jnp.float32)
        grads_rows = lax.dynamic_slice_in_dim(basis_grads, start, rblock, 0).reshape(trows, TILE, B, H).astype(jnp.float32)
        grads_k = jnp.take(grads_rows, trs, axis=0)
        gram = jnp.einsum("kih,kibh->kb", messages.astype(jnp.float32), grads_k) * live[:, None]
        pick_rel = (rels[:, None] == jnp.arange(R, dtype=jnp.int32)[None, :]).astype(jnp.float32)
        dcoef_acc = dcoef_acc + jnp.dot(pick_rel.T, gram, precision=lax.Precision.HIGHEST)
        mixed = jnp.einsum("kb,kibh->kih", coef_k, grads_k).astype(jnp.bfloat16)
        back = jnp.einsum("kij,kih->kjh", values, mixed.astype(jnp.float32))
        select_column = (tile_column_slice[:, None] == jnp.arange(tile_column_list, dtype=jnp.int32)[None, :]).astype(jnp.float32)
        dx_part = jnp.einsum("kc,kjh->cjh", select_column, back, precision=lax.Precision.HIGHEST).reshape(cblock, H)
        cstart = (colidx * cblock).astype(jnp.int32)
        dx_acc = lax.dynamic_update_slice_in_dim(dx_acc, lax.dynamic_slice_in_dim(dx_acc, cstart, cblock, 0) + dx_part, cstart, 0)
        return (out_acc, dv_acc, dcoef_acc, dx_acc), None

    init = (jnp.zeros((classes, H), jnp.float32), jnp.zeros((B * H, H), jnp.float32), jnp.zeros((R, B), jnp.float32), jnp.zeros((classes, H), jnp.float32))
    (out_acc, dv_acc, dcoef_acc, dx_acc), unused = lax.scan(per_device, init, jnp.arange(devices, dtype=jnp.int32))
    scale = classes ** -0.5
    layer_out = out_acc.astype(jnp.bfloat16)
    grad_bases = (dv_acc * scale).reshape(B, H, H)
    grad_coef = dcoef_acc * scale
    quotient = dx_acc / counts[:, None]
    grad_entities = jnp.take(quotient, owner, axis=0)
    return (layer_out, grad_entities, grad_bases, grad_coef)
```

```python
import jax
import jax.numpy as jnp
from jax import lax
from jax.experimental import pallas as pl
from jax.experimental.pallas import tpu as pltpu
from jax.sharding import Mesh
from jax.sharding import PartitionSpec as P

NY, NZ, NC, NX = 4, 8, 2, 4
TILE = 128
H = 256
B = 8
SLOTS = 32
TROWS = 4
RELS = 500
F32, BF16 = jnp.float32, jnp.bfloat16
ROWS = ("y", "z", "c")
DEVICES = ("y", "z", "c", "x")
VMEM = pl.BlockSpec(memory_space=pltpu.VMEM)
SMEM = pl.BlockSpec(memory_space=pltpu.SMEM)
ANY = pl.BlockSpec(memory_space=pl.ANY)
PARAMS = pltpu.CompilerParams(vmem_limit_bytes=56 * 2**20)


def backward_kernel(
    trow, dslot, count, coef, cot, bases, tiles, grads, keep, give, total, mixed
):
    for t in range(TROWS):
        for b in range(B):
            g = lax.dot_general(
                cot[pl.ds(t * TILE, TILE), :],
                bases[pl.ds(b * H, H), :],
                (((1,), (1,)), ((), ())),
                preferred_element_type=F32,
            )
            grads[t, :, pl.ds(b * H, H)] = g.astype(BF16)
    total[...] = jnp.zeros_like(total)

    def turn(s, carry):
        t = trow[s]
        d = dslot[s]
        for r in range(4):
            rows = pl.ds(r * 32, 32)
            acc = coef[s, 0] * grads[t, rows, pl.ds(0, H)].astype(F32)
            for b in range(1, B):
                acc = acc + coef[s, b] * grads[t, rows, pl.ds(b * H, H)].astype(F32)
            mixed[rows, :] = acc.astype(BF16)
        back = lax.dot_general(
            tiles[s], mixed[...], (((0,), (0,)), ((), ())), preferred_element_type=F32
        )
        total[d] = total[d] + back
        return carry

    lax.fori_loop(0, count[0], turn, 0)
    keep[...] = total[pl.ds(0, SLOTS)]
    give[...] = total[pl.ds(SLOTS, SLOTS)].astype(BF16)


def backward(trow, dslot, count, coef, cot_rows, stacked, tile_values):
    blocks = (SLOTS, TILE, H)
    return pl.pallas_call(
        backward_kernel,
        in_specs=[SMEM, SMEM, SMEM, SMEM, VMEM, VMEM, VMEM],
        out_specs=[VMEM, VMEM, VMEM],
        out_shape=[
            jax.ShapeDtypeStruct((TROWS, TILE, B * H), BF16),
            jax.ShapeDtypeStruct(blocks, F32),
            jax.ShapeDtypeStruct(blocks, BF16),
        ],
        scratch_shapes=[
            pltpu.VMEM((2 * SLOTS, TILE, H), F32),
            pltpu.VMEM((TILE, H), BF16),
        ],
        compiler_params=PARAMS,
        name="backward",
    )(trow, dslot, count, coef, cot_rows, stacked, tile_values)


def forward_kernel(
    trow, xslot, count, half, coef, relc, relr, xmine, xother, tiles, grads, bases, cot,
    outp, dkeep, dgive, coefg,
    feats, sums, part, dv, msg, gram, sems,
):
    copies = [
        pltpu.make_async_copy(src, feats.at[pl.ds(k * SLOTS, SLOTS)], sems.at[k])
        for k, src in enumerate((xmine, xother))
    ]
    for copy in copies:
        copy.start()
    sums[...] = jnp.zeros_like(sums)
    gram[...] = jnp.zeros_like(gram)
    for copy in copies:
        copy.wait()

    def turn(s, carry):
        t = trow[s]
        m = jnp.dot(tiles[s], feats[xslot[s]], preferred_element_type=F32)
        msg[...] = m.astype(BF16).astype(F32)
        dots = [jnp.zeros((8, 128), F32) for _ in range(B)]
        for r in range(4):
            rows = pl.ds(r * 32, 32)
            mm = msg[rows, :]
            for b in range(B):
                cols = pl.ds(b * H, H)
                sums[t, rows, cols] = sums[t, rows, cols] + coef[s, b] * mm
                prod = mm * grads[t, rows, cols].astype(F32)
                fold = jnp.sum(prod.reshape(4, 8, H), axis=0)
                dots[b] = dots[b] + (fold[:, :128] + fold[:, 128:])
        for b in range(B):
            gram[s, b] = dots[b]
        return carry

    lax.fori_loop(0, count[0], turn, 0)

    for t in range(TROWS):
        part[t] = sums[t].astype(BF16)
        outp[t] = jnp.dot(part[t], bases[...], preferred_element_type=F32).astype(BF16)
    for b in range(B):
        acc = None
        for t in range(TROWS):
            d = lax.dot_general(
                part[t, :, pl.ds(b * H, H)],
                cot[pl.ds(t * TILE, TILE), :],
                (((0,), (0,)), ((), ())),
                preferred_element_type=F32,
            )
            acc = d if acc is None else acc + d
        dv[b // 4, pl.ds((b % 4) * H, H), :] = acc
    mine = half[0]
    dkeep[...] = dv[mine]
    dgive[pl.ds(0, 1024), :] = dv[1 - mine].astype(BF16)

    col = jnp.sum(jnp.sum(gram[...].reshape(SLOTS * B, 8, 128), axis=1), axis=1, keepdims=True)
    lane = lax.broadcasted_iota(jnp.int32, (SLOTS * B, 128), 1)
    row = lax.broadcasted_iota(jnp.int32, (SLOTS * B, 128), 0)
    pick = (lane % B == row % B) & (lane // B == relc[...] % 16)
    spread = jnp.where(pick, col, 0.0)
    line = lax.broadcasted_iota(jnp.int32, (32, SLOTS * B), 0)
    gather = (relr[...] // 16 == line).astype(F32)
    cg = jnp.dot(gather, spread, precision=lax.Precision.HIGHEST, preferred_element_type=F32)
    coefg[...] = cg
    hi = cg.astype(BF16)
    dgive[pl.ds(1024, 32), pl.ds(0, 128)] = hi
    dgive[pl.ds(1024, 32), pl.ds(128, 128)] = (cg - hi.astype(F32)).astype(BF16)


def forward(trow, xslot, count, half, coef, relc, relr, xmine, xother, tiles, grads, stacked, cot_rows):
    return pl.pallas_call(
        forward_kernel,
        in_specs=[SMEM] * 5 + [VMEM] * 2 + [ANY] * 2 + [VMEM] * 4,
        out_specs=[VMEM] * 4,
        out_shape=[
            jax.ShapeDtypeStruct((TROWS, TILE, H), BF16),
            jax.ShapeDtypeStruct((1024, H), F32),
            jax.ShapeDtypeStruct((1056, H), BF16),
            jax.ShapeDtypeStruct((32, 128), F32),
        ],
        scratch_shapes=[
            pltpu.VMEM((2 * SLOTS, TILE, H), BF16),
            pltpu.VMEM((TROWS, TILE, B * H), F32),
            pltpu.VMEM((TROWS, TILE, B * H), BF16),
            pltpu.VMEM((2, 1024, H), F32),
            pltpu.VMEM((TILE, H), F32),
            pltpu.VMEM((SLOTS, B, 8, 128), F32),
            pltpu.SemaphoreType.DMA((2,)),
        ],
        compiler_params=PARAMS,
        name="forward",
    )(trow, xslot, count, half, coef, relc, relr, xmine, xother, tiles, grads, stacked, cot_rows)


def swap(x):
    return lax.ppermute(x, "c", [(0, 1), (1, 0)])


def exchange(x, axes):
    return lax.all_to_all(x, axes, split_axis=0, concat_axis=0, tiled=True)


def spread_to(x, axes, n):
    return exchange(jnp.broadcast_to(x[None], (n,) + x.shape), axes)


def two_parts(x):
    hi = lax.reduce_precision(x, 8, 7)
    return jnp.concatenate([hi, x - hi], axis=-1).astype(BF16)


def after(x, y):
    return lax.optimization_barrier((x, y))


def local(
    entity_feats,
    class_map,
    tile_values,
    tile_rows,
    tile_column_index,
    tile_rels,
    tile_counts,
    coefficients,
    bases,
    cotangent,
):
    mine = lax.axis_index("c").astype(jnp.int32)
    member = class_map[:, None] == jnp.arange(TILE, dtype=jnp.int32)[None, :]
    sums = lax.dot_general(
        member.astype(BF16), entity_feats, (((0,), (0,)), ((), ())), preferred_element_type=F32
    )
    counts = jnp.sum(member.astype(F32), axis=0)
    class_feat = (sums / counts[:, None]).astype(BF16)

    pick_rel = (tile_rels[:, None] == jnp.arange(RELS, dtype=jnp.int32)[None, :]).astype(BF16)
    coef = jnp.dot(pick_rel, coefficients, preferred_element_type=F32)
    other = (tile_column_index % 2 != mine).astype(jnp.int32) * SLOTS
    ty = tile_column_index // (2 * NZ)
    tz = (tile_column_index // 2) % NZ
    xslot = other + ty * NZ + tz
    dslot = other + tz * NY + ty
    stacked = bases.reshape(B * H, H)

    with jax.named_scope("feats_z"):
        feats_z = spread_to(class_feat, "z", NZ).reshape(NZ * TILE, H)
    cotangent, feats_z = after(cotangent, feats_z)
    with jax.named_scope("feats_y"):
        feats_mine = lax.all_gather(feats_z, "y", axis=0, tiled=True)
    with jax.named_scope("cot_x"):
        cot_rows = lax.all_gather(cotangent, "x", axis=0, tiled=True)

    grads, keep, give = backward(
        tile_rows, dslot, tile_counts, coef, cot_rows, stacked, tile_values
    )
    with jax.named_scope("dx_c"):
        got = swap(give)
    dx = (keep + got.astype(F32)).reshape(NZ * NY * TILE, H)
    with jax.named_scope("dx_z"):
        dx = lax.psum_scatter(dx, "z", scatter_dimension=0, tiled=True)
    with jax.named_scope("dx_y"):
        dx = lax.psum_scatter(dx, "y", scatter_dimension=0, tiled=True)

    feats_mine = feats_mine.reshape(SLOTS, TILE, H)
    with jax.named_scope("feats_c"):
        feats_other = swap(feats_mine)
    rels = jnp.repeat(tile_rels, B)
    outp, dkeep, dgive, coefg = forward(
        tile_rows, xslot, tile_counts, mine[None], coef, rels[:, None], rels[None, :],
        feats_mine, feats_other, tile_values, grads, stacked, cot_rows,
    )

    with jax.named_scope("dv_c"):
        dgot = swap(dgive)
    dv = (dkeep + dgot[:1024].astype(F32)).reshape(NX, 256, H).astype(BF16)
    cg = coefg + dgot[1024:, :128].astype(F32) + dgot[1024:, 128:].astype(F32)
    cg_x = jnp.broadcast_to(two_parts(cg)[None], (NX, 32, H))
    with jax.named_scope("dv_x"):
        got_x = exchange(jnp.concatenate([dv, outp, cg_x], axis=1), "x")
    sum_x = jnp.sum(got_x.astype(F32), axis=0)
    layer_out = sum_x[256:384].astype(BF16)
    cg = sum_x[384:, :128] + sum_x[384:, 128:]
    pad = jnp.zeros((NY * NZ, 7, H), BF16)
    packed = jnp.concatenate(
        [sum_x[:256].reshape(NY * NZ, 8, H).astype(BF16), two_parts(cg)[:, None, :], pad], axis=1
    )
    with jax.named_scope("dv_yz"):
        got_yz = exchange(packed, ("y", "z"))
    sum_yz = jnp.sum(got_yz.astype(F32), axis=0)
    cg = sum_yz[8:9, :128] + sum_yz[8:9, 128:]
    packed = jnp.concatenate(
        [sum_yz[:8].astype(BF16), two_parts(cg), jnp.zeros((7, H), BF16)], axis=0
    )
    with jax.named_scope("all_yz"):
        all_yz = spread_to(packed, ("y", "z"), NY * NZ)
    scale = (NY * NZ * NC * NX * TILE) ** (-0.5)
    cg = all_yz[:, 8, :128].astype(F32) + all_yz[:, 8, 128:].astype(F32)
    grad_coef = (cg * scale).reshape(512, B)[:RELS]
    with jax.named_scope("all_x"):
        all_x = spread_to(all_yz[:, :8].reshape(256, H), "x", NX).reshape(1024, H)
    with jax.named_scope("all_c"):
        all_other = swap(all_x)
    first = jnp.where(mine == 0, all_x, all_other)
    second = jnp.where(mine == 0, all_other, all_x)
    grad_bases = (jnp.stack([first, second]).astype(F32) * scale).reshape(B, H, H)

    quotient = dx / counts[:, None]
    grad_entities = jnp.dot(member.astype(F32), quotient, precision=lax.Precision.HIGHEST)
    return (layer_out, grad_entities, grad_bases, grad_coef)


def solution(mesh):
    grid = Mesh(mesh.devices.reshape(NY, NZ, NC, NX), DEVICES)
    by_tile = P(DEVICES)
    by_class = P(("x",) + ROWS)
    placed = (
        by_class,
        by_class,
        by_tile,
        by_tile,
        by_tile,
        by_tile,
        by_tile,
        P(),
        P(),
        by_tile,
    )
    return jax.shard_map(
        local,
        mesh=grid,
        in_specs=placed,
        out_specs=(by_tile, by_class, P(), P()),
        check_vma=False,
    )
```

```python
import jax
import jax.numpy as jnp
from jax import lax
from jax.experimental import pallas as pl
from jax.experimental.pallas import tpu as pltpu
from jax.sharding import Mesh
from jax.sharding import PartitionSpec as P

NY, NZ, NC, NX = 4, 8, 2, 4
TILE = 128
H = 256
B = 8
SLOTS = 32
TROWS = 4
RELS = 500
F32, BF16 = jnp.float32, jnp.bfloat16
ROWS = ("y", "z", "c")
DEVICES = ("y", "z", "c", "x")
VMEM = pl.BlockSpec(memory_space=pltpu.VMEM)
SMEM = pl.BlockSpec(memory_space=pltpu.SMEM)
ANY = pl.BlockSpec(memory_space=pl.ANY)
PARAMS = pltpu.CompilerParams(vmem_limit_bytes=56 * 2**20)


def by_row(trow, count, order, filled):
    for t in range(TROWS):
        filled[t] = 0

    def put(s, carry):
        t = trow[s]
        n = filled[t]
        order[t, n] = s
        filled[t] = n + 1
        return carry

    lax.fori_loop(0, count[0], put, 0)
    for t in range(TROWS):
        order[t, filled[t]] = SLOTS


def pairs(order, filled, body):
    def row(t, carry):
        def pair(p, inner):
            body(t, order[t, 2 * p], order[t, 2 * p + 1])
            return inner

        lax.fori_loop(0, (filled[t] + 1) // 2, pair, 0)
        return carry

    lax.fori_loop(0, TROWS, row, 0)


def fold(x):
    return (x[:8, :128] + x[:8, 128:]) + (x[8:, :128] + x[8:, 128:])


def fours(count, body):
    def group(q, carry):
        for k in range(4):
            body(4 * q + k)
        return carry

    lax.fori_loop(0, (count[0] + 3) // 4, group, 0)


def backward_kernel(
    trow, dslot, count, coef, cot_in, bases_in, tiles_in, grads_out, keep_out, give_out,
    cot, bases, tiles, wide, grads, total, mixed, narrow, order, filled, sems,
):
    loads = [
        pltpu.make_async_copy(src, dst, sems.at[k])
        for k, (src, dst) in enumerate(((cot_in, cot), (bases_in, bases), (tiles_in, tiles)))
    ]
    for copy in loads:
        copy.start()
    total[...] = jnp.zeros_like(total)
    mixed[...] = jnp.zeros_like(mixed)
    by_row(trow, count, order, filled)
    loads[0].wait()
    loads[1].wait()
    for b in range(B):
        g = lax.dot_general(
            cot[...], bases[pl.ds(b * H, H), :], (((1,), (1,)), ((), ())), preferred_element_type=F32
        ).astype(BF16)
        grads[:, b] = g.reshape(TROWS, TILE, H)
        wide[:, b] = g.astype(F32).reshape(TROWS, TILE, H)
    store = pltpu.make_async_copy(grads, grads_out, sems.at[3])
    store.start()

    def mix(t, s1, s2):
        c1 = [coef[s1, b] for b in range(B)]
        c2 = [coef[s2, b] for b in range(B)]
        for r in range(4):
            rows = pl.ds(r * 32, 32)
            g = wide[t, 0, rows, :]
            m1 = c1[0] * g
            m2 = c2[0] * g
            for b in range(1, B):
                g = wide[t, b, rows, :]
                m1 = m1 + c1[b] * g
                m2 = m2 + c2[b] * g
            mixed[s1, rows, :] = m1.astype(BF16)
            mixed[s2, rows, :] = m2.astype(BF16)

    pairs(order, filled, mix)
    loads[2].wait()

    def back(s):
        d = dslot[s]
        total[d] = total[d] + lax.dot_general(
            tiles[s], mixed[s], (((0,), (0,)), ((), ())), preferred_element_type=F32
        )

    fours(count, back)
    outs = []
    for k, out in ((1, give_out), (0, keep_out)):
        narrow[k] = total[pl.ds(k * SLOTS, SLOTS)].astype(BF16)
        copy = pltpu.make_async_copy(narrow.at[k], out, sems.at[4 + k])
        copy.start()
        outs.append(copy)
    store.wait()
    for copy in outs:
        copy.wait()


def backward(trow, dslot, count, coef, cot_rows, stacked, tile_values):
    blocks = jax.ShapeDtypeStruct((SLOTS, TILE, H), BF16)
    return pl.pallas_call(
        backward_kernel,
        in_specs=[SMEM] * 4 + [ANY] * 3,
        out_specs=[ANY] * 3,
        out_shape=[jax.ShapeDtypeStruct((TROWS, B, TILE, H), BF16), blocks, blocks],
        scratch_shapes=[
            pltpu.VMEM((TROWS * TILE, H), BF16),
            pltpu.VMEM((B * H, H), BF16),
            pltpu.VMEM((SLOTS, TILE, TILE), BF16),
            pltpu.VMEM((TROWS, B, TILE, H), F32),
            pltpu.VMEM((TROWS, B, TILE, H), BF16),
            pltpu.VMEM((2 * SLOTS, TILE, H), F32),
            pltpu.VMEM((SLOTS + 1, TILE, H), BF16),
            pltpu.VMEM((2, SLOTS, TILE, H), BF16),
            pltpu.SMEM((TROWS, SLOTS + 8), jnp.int32),
            pltpu.SMEM((TROWS,), jnp.int32),
            pltpu.SemaphoreType.DMA((6,)),
        ],
        compiler_params=PARAMS,
        name="backward",
    )(trow, dslot, count, coef, cot_rows, stacked, tile_values)


def forward_kernel(
    trow, xslot, count, half, coef, relc, relr, xmine, xother, tiles_in, grads_in, bases_in, cot_in,
    outp, dkeep, dgive, coefg,
    feats, tiles, grads, bases, cot, sums, part, msg, gram, order, filled, sems,
):
    loads = [
        pltpu.make_async_copy(src, dst, sems.at[k])
        for k, (src, dst) in enumerate(
            (
                (tiles_in, tiles),
                (xmine, feats.at[pl.ds(0, SLOTS)]),
                (xother, feats.at[pl.ds(SLOTS, SLOTS)]),
                (grads_in, grads),
                (bases_in, bases),
                (cot_in, cot),
            )
        )
    ]
    for copy in loads:
        copy.start()
    sums[...] = jnp.zeros_like(sums)
    msg[SLOTS] = jnp.zeros((TILE, H), F32)
    gram[...] = jnp.zeros_like(gram)
    by_row(trow, count, order, filled)
    for copy in loads[:4]:
        copy.wait()
    def message(s):
        m = jnp.dot(tiles[s], feats[xslot[s]], preferred_element_type=F32).astype(BF16)
        msg[s] = m.astype(F32)

    fours(count, message)

    def add(t, s1, s2):
        c1 = [coef[s1, b] for b in range(B)]
        c2 = [coef[s2, b] for b in range(B)]
        d1 = [jnp.zeros((8, 128), F32)] * B
        d2 = [jnp.zeros((8, 128), F32)] * B
        for r in range(8):
            rows = pl.ds(r * 16, 16)
            m1 = msg[s1, rows, :]
            m2 = msg[s2, rows, :]
            for b in range(B):
                sums[t, b, rows, :] = sums[t, b, rows, :] + (c1[b] * m1 + c2[b] * m2)
                g = grads[t, b, rows, :].astype(F32)
                d1[b] = d1[b] + fold(m1 * g)
                d2[b] = d2[b] + fold(m2 * g)
        for b in range(B):
            gram[s1, b] = d1[b]
            gram[s2, b] = d2[b]

    pairs(order, filled, add)

    for copy in loads[4:]:
        copy.wait()
    for t in range(TROWS):
        for b in range(B):
            part[pl.ds(t * TILE, TILE), pl.ds(b * H, H)] = sums[t, b].astype(BF16)
    outp[...] = jnp.dot(part[...], bases[...], preferred_element_type=F32).astype(BF16)
    mine = half[0]

    def outer(k):
        cols = pl.ds(pl.multiple_of(k * H, H), H)
        return lax.dot_general(
            part[:, cols], cot[...], (((0,), (0,)), ((), ())), preferred_element_type=F32
        )

    for k in range(B // 2):
        rows = pl.ds(k * H, H)
        dkeep[rows, :] = outer(mine * (B // 2) + k)
        dgive[rows, :] = outer((1 - mine) * (B // 2) + k).astype(BF16)

    col = jnp.sum(jnp.sum(gram[pl.ds(0, SLOTS)].reshape(SLOTS * B, 8, 128), axis=1), axis=1, keepdims=True)
    lane = lax.broadcasted_iota(jnp.int32, (SLOTS * B, 128), 1)
    row = lax.broadcasted_iota(jnp.int32, (SLOTS * B, 128), 0)
    pick = (lane % B == row % B) & (lane // B == relc[...] % 16) & (row < count[0] * B)
    spread = jnp.where(pick, col, 0.0)
    line = lax.broadcasted_iota(jnp.int32, (32, SLOTS * B), 0)
    gather = (relr[...] // 16 == line).astype(F32)
    cg = jnp.dot(gather, spread, precision=lax.Precision.HIGHEST, preferred_element_type=F32)
    coefg[...] = cg
    hi = cg.astype(BF16)
    dgive[pl.ds(1024, 32), pl.ds(0, 128)] = hi
    dgive[pl.ds(1024, 32), pl.ds(128, 128)] = (cg - hi.astype(F32)).astype(BF16)


def forward(trow, xslot, count, half, coef, relc, relr, xmine, xother, tiles, grads, stacked, cot_rows):
    return pl.pallas_call(
        forward_kernel,
        in_specs=[SMEM] * 5 + [VMEM] * 2 + [ANY] * 6,
        out_specs=[VMEM] * 4,
        out_shape=[
            jax.ShapeDtypeStruct((TROWS * TILE, H), BF16),
            jax.ShapeDtypeStruct((1024, H), F32),
            jax.ShapeDtypeStruct((1056, H), BF16),
            jax.ShapeDtypeStruct((32, 128), F32),
        ],
        scratch_shapes=[
            pltpu.VMEM((2 * SLOTS, TILE, H), BF16),
            pltpu.VMEM((SLOTS, TILE, TILE), BF16),
            pltpu.VMEM((TROWS, B, TILE, H), BF16),
            pltpu.VMEM((B * H, H), BF16),
            pltpu.VMEM((TROWS * TILE, H), BF16),
            pltpu.VMEM((TROWS, B, TILE, H), F32),
            pltpu.VMEM((TROWS * TILE, B * H), BF16),
            pltpu.VMEM((SLOTS + 1, TILE, H), F32),
            pltpu.VMEM((SLOTS + 1, B, 8, 128), F32),
            pltpu.SMEM((TROWS, SLOTS + 8), jnp.int32),
            pltpu.SMEM((TROWS,), jnp.int32),
            pltpu.SemaphoreType.DMA((6,)),
        ],
        compiler_params=PARAMS,
        name="forward",
    )(trow, xslot, count, half, coef, relc, relr, xmine, xother, tiles, grads, stacked, cot_rows)


def swap(x):
    return lax.ppermute(x, "c", [(0, 1), (1, 0)])


def exchange(x, axes):
    return lax.all_to_all(x, axes, split_axis=0, concat_axis=0, tiled=True)


def spread_to(x, axes, n):
    return exchange(jnp.broadcast_to(x[None], (n,) + x.shape), axes)


def two_parts(x):
    hi = lax.reduce_precision(x, 8, 7)
    return jnp.concatenate([hi, x - hi], axis=-1).astype(BF16)


def after(x, y):
    return lax.optimization_barrier((x, y))


def local(
    entity_feats,
    class_map,
    tile_values,
    tile_rows,
    tile_column_index,
    tile_rels,
    tile_counts,
    coefficients,
    bases,
    cotangent,
):
    mine = lax.axis_index("c").astype(jnp.int32)
    member = class_map[:, None] == jnp.arange(TILE, dtype=jnp.int32)[None, :]
    sums = lax.dot_general(
        member.astype(BF16), entity_feats, (((0,), (0,)), ((), ())), preferred_element_type=F32
    )
    counts = jnp.sum(member.astype(F32), axis=0)
    class_feat = (sums / counts[:, None]).astype(BF16)

    rels = jnp.pad(tile_rels, (0, 8), constant_values=-1)
    pick_rel = (rels[:, None] == jnp.arange(RELS, dtype=jnp.int32)[None, :]).astype(BF16)
    coef = jnp.dot(pick_rel, coefficients, preferred_element_type=F32)
    other = (tile_column_index % 2 != mine).astype(jnp.int32) * SLOTS
    ty = tile_column_index // (2 * NZ)
    tz = (tile_column_index // 2) % NZ
    xslot = other + ty * NZ + tz
    dslot = other + tz * NY + ty
    stacked = bases.reshape(B * H, H)

    with jax.named_scope("feats_z"):
        feats_z = spread_to(class_feat, "z", NZ).reshape(NZ * TILE, H)
    cotangent, feats_z = after(cotangent, feats_z)
    with jax.named_scope("feats_y"):
        feats_mine = lax.all_gather(feats_z, "y", axis=0, tiled=True)
    with jax.named_scope("cot_x"):
        cot_rows = lax.all_gather(cotangent, "x", axis=0, tiled=True)

    grads, keep, give = backward(
        tile_rows, dslot, tile_counts, coef, cot_rows, stacked, tile_values
    )
    with jax.named_scope("dx_c"):
        got = swap(give)
    dx = (keep.astype(F32) + got.astype(F32)).reshape(NZ * NY * TILE, H)
    with jax.named_scope("dx_z"):
        dx = lax.psum_scatter(dx, "z", scatter_dimension=0, tiled=True)
    feats_mine = feats_mine.reshape(SLOTS, TILE, H)
    with jax.named_scope("feats_c"):
        feats_other = swap(feats_mine)
    rels = jnp.repeat(tile_rels, B)
    outp, dkeep, dgive, coefg = forward(
        tile_rows, xslot, tile_counts, mine[None], coef, rels[:, None], rels[None, :],
        feats_mine, feats_other, tile_values, grads, stacked, cot_rows,
    )

    with jax.named_scope("dv_c"):
        dgot = swap(dgive)
    dv = (dkeep + dgot[:1024].astype(F32)).reshape(NX, 256, H).astype(BF16)
    cg = coefg + dgot[1024:, :128].astype(F32) + dgot[1024:, 128:].astype(F32)
    cg_x = jnp.broadcast_to(two_parts(cg)[None], (NX, 32, H))
    with jax.named_scope("dv_x"):
        got_x = exchange(jnp.concatenate([dv, outp.reshape(NX, TILE, H), cg_x], axis=1), "x")
    sum_x = jnp.sum(got_x.astype(F32), axis=0)
    layer_out = sum_x[256:384].astype(BF16)
    cg = sum_x[384:, :128] + sum_x[384:, 128:]
    pad = jnp.zeros((NY * NZ, 7, H), BF16)
    packed = jnp.concatenate(
        [sum_x[:256].reshape(NY * NZ, 8, H).astype(BF16), two_parts(cg)[:, None, :], pad], axis=1
    )
    with jax.named_scope("dv_yz"):
        got_yz = exchange(packed, ("y", "z"))
    sum_yz = jnp.sum(got_yz.astype(F32), axis=0)
    cg = sum_yz[8:9, :128] + sum_yz[8:9, 128:]
    packed = jnp.concatenate(
        [sum_yz[:8].astype(BF16), two_parts(cg), jnp.zeros((7, H), BF16)], axis=0
    )
    packed, dx = after(packed, dx)
    with jax.named_scope("dx_y"):
        dx = lax.psum_scatter(dx, "y", scatter_dimension=0, tiled=True)
    with jax.named_scope("all_yz"):
        all_yz = spread_to(packed, ("y", "z"), NY * NZ)
    scale = (NY * NZ * NC * NX * TILE) ** (-0.5)
    cg = all_yz[:, 8, :128].astype(F32) + all_yz[:, 8, 128:].astype(F32)
    grad_coef = (cg * scale).reshape(512, B)[:RELS]
    with jax.named_scope("all_x"):
        all_x = spread_to(all_yz[:, :8].reshape(256, H), "x", NX).reshape(1024, H)
    with jax.named_scope("all_c"):
        all_other = swap(all_x)
    first = jnp.where(mine == 0, all_x, all_other)
    second = jnp.where(mine == 0, all_other, all_x)
    grad_bases = (jnp.stack([first, second]).astype(F32) * scale).reshape(B, H, H)

    quotient = dx / counts[:, None]
    grad_entities = jnp.dot(member.astype(F32), quotient, precision=lax.Precision.HIGHEST)
    return (layer_out, grad_entities, grad_bases, grad_coef)


def solution(mesh):
    grid = Mesh(mesh.devices.reshape(NY, NZ, NC, NX), DEVICES)
    by_tile = P(DEVICES)
    by_class = P(("x",) + ROWS)
    placed = (
        by_class,
        by_class,
        by_tile,
        by_tile,
        by_tile,
        by_tile,
        by_tile,
        P(),
        P(),
        by_tile,
    )
    return jax.shard_map(
        local,
        mesh=grid,
        in_specs=placed,
        out_specs=(by_tile, by_class, P(), P()),
        check_vma=False,
    )
```

```python
import jax
import jax.numpy as jnp
from jax import lax
from jax.experimental import pallas as pl
from jax.experimental.pallas import tpu as pltpu
from jax.sharding import Mesh
from jax.sharding import PartitionSpec as P

NY, NZ, NC, NX = 4, 8, 2, 4
TILE = 128
H = 256
B = 8
SLOTS = 32
TROWS = 4
RELS = 500
F32, BF16 = jnp.float32, jnp.bfloat16
ROWS = ("y", "z", "c")
DEVICES = ("y", "z", "c", "x")
VMEM = pl.BlockSpec(memory_space=pltpu.VMEM)
SMEM = pl.BlockSpec(memory_space=pltpu.SMEM)
ANY = pl.BlockSpec(memory_space=pl.ANY)
PARAMS = pltpu.CompilerParams(vmem_limit_bytes=56 * 2**20)


def by_row(trow, count, order, filled):
    for t in range(TROWS):
        filled[t] = 0

    def put(s, carry):
        t = trow[s]
        n = filled[t]
        order[t, n] = s
        filled[t] = n + 1
        return carry

    lax.fori_loop(0, count[0], put, 0)
    for t in range(TROWS):
        order[t, filled[t]] = SLOTS


def pairs(order, filled, body):
    def row(t, carry):
        def pair(p, inner):
            body(t, order[t, 2 * p], order[t, 2 * p + 1])
            return inner

        lax.fori_loop(0, (filled[t] + 1) // 2, pair, 0)
        return carry

    lax.fori_loop(0, TROWS, row, 0)


def fold(x):
    return (x[:8, :128] + x[:8, 128:]) + (x[8:, :128] + x[8:, 128:])


def fours(count, body):
    def group(q, carry):
        for k in range(4):
            body(4 * q + k)
        return carry

    lax.fori_loop(0, (count[0] + 3) // 4, group, 0)


def backward_kernel(
    trow, dslot, count, coef, cot_in, bases_in, tiles_in, grads_out, keep_out, give_out,
    cot, bases, tiles, wide, grads, total, mixed, narrow, order, filled, sems,
):
    loads = [
        pltpu.make_async_copy(src, dst, sems.at[k])
        for k, (src, dst) in enumerate(((cot_in, cot), (bases_in, bases), (tiles_in, tiles)))
    ]
    for copy in loads:
        copy.start()
    total[...] = jnp.zeros_like(total)
    mixed[...] = jnp.zeros_like(mixed)
    by_row(trow, count, order, filled)
    loads[0].wait()
    loads[1].wait()
    for b in range(B):
        g = lax.dot_general(
            cot[...], bases[pl.ds(b * H, H), :], (((1,), (1,)), ((), ())), preferred_element_type=F32
        ).astype(BF16)
        grads[:, b] = g.reshape(TROWS, TILE, H)
        wide[:, b] = g.astype(F32).reshape(TROWS, TILE, H)
    store = pltpu.make_async_copy(grads, grads_out, sems.at[3])
    store.start()

    def mix(t, s1, s2):
        c1 = [coef[s1, b] for b in range(B)]
        c2 = [coef[s2, b] for b in range(B)]
        for r in range(4):
            rows = pl.ds(r * 32, 32)
            g = wide[t, 0, rows, :]
            m1 = c1[0] * g
            m2 = c2[0] * g
            for b in range(1, B):
                g = wide[t, b, rows, :]
                m1 = m1 + c1[b] * g
                m2 = m2 + c2[b] * g
            mixed[s1, rows, :] = m1.astype(BF16)
            mixed[s2, rows, :] = m2.astype(BF16)

    pairs(order, filled, mix)
    loads[2].wait()

    def back(s):
        d = dslot[s]
        total[d] = total[d] + lax.dot_general(
            tiles[s], mixed[s], (((0,), (0,)), ((), ())), preferred_element_type=F32
        )

    fours(count, back)
    outs = []
    for k, out in ((1, give_out), (0, keep_out)):
        narrow[k] = total[pl.ds(k * SLOTS, SLOTS)].astype(BF16)
        copy = pltpu.make_async_copy(narrow.at[k], out, sems.at[4 + k])
        copy.start()
        outs.append(copy)
    store.wait()
    for copy in outs:
        copy.wait()


def backward(trow, dslot, count, coef, cot_rows, stacked, tile_values):
    blocks = jax.ShapeDtypeStruct((SLOTS, TILE, H), BF16)
    return pl.pallas_call(
        backward_kernel,
        in_specs=[SMEM] * 4 + [ANY] * 3,
        out_specs=[ANY] * 3,
        out_shape=[jax.ShapeDtypeStruct((TROWS, B, TILE, H), BF16), blocks, blocks],
        scratch_shapes=[
            pltpu.VMEM((TROWS * TILE, H), BF16),
            pltpu.VMEM((B * H, H), BF16),
            pltpu.VMEM((SLOTS, TILE, TILE), BF16),
            pltpu.VMEM((TROWS, B, TILE, H), F32),
            pltpu.VMEM((TROWS, B, TILE, H), BF16),
            pltpu.VMEM((2 * SLOTS, TILE, H), F32),
            pltpu.VMEM((SLOTS + 1, TILE, H), BF16),
            pltpu.VMEM((2, SLOTS, TILE, H), BF16),
            pltpu.SMEM((TROWS, SLOTS + 8), jnp.int32),
            pltpu.SMEM((TROWS,), jnp.int32),
            pltpu.SemaphoreType.DMA((6,)),
        ],
        compiler_params=PARAMS,
        name="backward",
    )(trow, dslot, count, coef, cot_rows, stacked, tile_values)


def forward_kernel(
    trow, xslot, count, half, coef, relc, relr, xmine, xother, tiles_in, grads_in, bases_in, cot_in,
    outp, dkeep, dgive, coefg,
    feats, tiles, grads, bases, cot, sums, part, msg, gram, order, filled, sems,
):
    loads = [
        pltpu.make_async_copy(src, dst, sems.at[k])
        for k, (src, dst) in enumerate(
            (
                (tiles_in, tiles),
                (xmine, feats.at[pl.ds(0, SLOTS)]),
                (xother, feats.at[pl.ds(SLOTS, SLOTS)]),
                (grads_in, grads),
                (bases_in, bases),
                (cot_in, cot),
            )
        )
    ]
    for copy in loads:
        copy.start()
    sums[...] = jnp.zeros_like(sums)
    msg[SLOTS] = jnp.zeros((TILE, H), F32)
    gram[...] = jnp.zeros_like(gram)
    by_row(trow, count, order, filled)
    for copy in loads[:4]:
        copy.wait()
    def message(s):
        m = jnp.dot(tiles[s], feats[xslot[s]], preferred_element_type=F32).astype(BF16)
        msg[s] = m.astype(F32)

    fours(count, message)

    def add(t, s1, s2):
        c1 = [coef[s1, b] for b in range(B)]
        c2 = [coef[s2, b] for b in range(B)]
        d1 = [jnp.zeros((8, 128), F32)] * B
        d2 = [jnp.zeros((8, 128), F32)] * B
        for r in range(8):
            rows = pl.ds(r * 16, 16)
            m1 = msg[s1, rows, :]
            m2 = msg[s2, rows, :]
            for b in range(B):
                sums[t, b, rows, :] = sums[t, b, rows, :] + (c1[b] * m1 + c2[b] * m2)
                g = grads[t, b, rows, :].astype(F32)
                d1[b] = d1[b] + fold(m1 * g)
                d2[b] = d2[b] + fold(m2 * g)
        for b in range(B):
            gram[s1, b] = d1[b]
            gram[s2, b] = d2[b]

    pairs(order, filled, add)

    for copy in loads[4:]:
        copy.wait()
    for t in range(TROWS):
        for b in range(B):
            part[pl.ds(t * TILE, TILE), pl.ds(b * H, H)] = sums[t, b].astype(BF16)
    outp[...] = jnp.dot(part[...], bases[...], preferred_element_type=F32).astype(BF16)
    mine = half[0]

    def outer(k):
        cols = pl.ds(pl.multiple_of(k * H, H), H)
        return lax.dot_general(
            part[:, cols], cot[...], (((0,), (0,)), ((), ())), preferred_element_type=F32
        )

    for k in range(B // 2):
        rows = pl.ds(k * H, H)
        dkeep[rows, :] = outer(mine * (B // 2) + k)
        dgive[rows, :] = outer((1 - mine) * (B // 2) + k).astype(BF16)

    col = jnp.sum(jnp.sum(gram[pl.ds(0, SLOTS)].reshape(SLOTS * B, 8, 128), axis=1), axis=1, keepdims=True)
    lane = lax.broadcasted_iota(jnp.int32, (SLOTS * B, 128), 1)
    row = lax.broadcasted_iota(jnp.int32, (SLOTS * B, 128), 0)
    pick = (lane % B == row % B) & (lane // B == relc[...] % 16) & (row < count[0] * B)
    spread = jnp.where(pick, col, 0.0)
    line = lax.broadcasted_iota(jnp.int32, (32, SLOTS * B), 0)
    gather = (relr[...] // 16 == line).astype(F32)
    cg = jnp.dot(gather, spread, precision=lax.Precision.HIGHEST, preferred_element_type=F32)
    coefg[...] = cg
    hi = cg.astype(BF16)
    dgive[pl.ds(1024, 32), pl.ds(0, 128)] = hi
    dgive[pl.ds(1024, 32), pl.ds(128, 128)] = (cg - hi.astype(F32)).astype(BF16)


def forward(trow, xslot, count, half, coef, relc, relr, xmine, xother, tiles, grads, stacked, cot_rows):
    return pl.pallas_call(
        forward_kernel,
        in_specs=[SMEM] * 5 + [VMEM] * 2 + [ANY] * 6,
        out_specs=[VMEM] * 4,
        out_shape=[
            jax.ShapeDtypeStruct((TROWS * TILE, H), BF16),
            jax.ShapeDtypeStruct((1024, H), F32),
            jax.ShapeDtypeStruct((1056, H), BF16),
            jax.ShapeDtypeStruct((32, 128), F32),
        ],
        scratch_shapes=[
            pltpu.VMEM((2 * SLOTS, TILE, H), BF16),
            pltpu.VMEM((SLOTS, TILE, TILE), BF16),
            pltpu.VMEM((TROWS, B, TILE, H), BF16),
            pltpu.VMEM((B * H, H), BF16),
            pltpu.VMEM((TROWS * TILE, H), BF16),
            pltpu.VMEM((TROWS, B, TILE, H), F32),
            pltpu.VMEM((TROWS * TILE, B * H), BF16),
            pltpu.VMEM((SLOTS + 1, TILE, H), F32),
            pltpu.VMEM((SLOTS + 1, B, 8, 128), F32),
            pltpu.SMEM((TROWS, SLOTS + 8), jnp.int32),
            pltpu.SMEM((TROWS,), jnp.int32),
            pltpu.SemaphoreType.DMA((6,)),
        ],
        compiler_params=PARAMS,
        name="forward",
    )(trow, xslot, count, half, coef, relc, relr, xmine, xother, tiles, grads, stacked, cot_rows)


def swap(x):
    return lax.ppermute(x, "c", [(0, 1), (1, 0)])


def exchange(x, axes):
    return lax.all_to_all(x, axes, split_axis=0, concat_axis=0, tiled=True)


def spread_to(x, axes, n):
    return exchange(jnp.broadcast_to(x[None], (n,) + x.shape), axes)


def two_parts(x):
    hi = lax.reduce_precision(x, 8, 7)
    return jnp.concatenate([hi, x - hi], axis=-1).astype(BF16)


def after(x, y):
    return lax.optimization_barrier((x, y))


def local(
    entity_feats,
    class_map,
    tile_values,
    tile_rows,
    tile_column_index,
    tile_rels,
    tile_counts,
    coefficients,
    bases,
    cotangent,
):
    mine = lax.axis_index("c").astype(jnp.int32)
    member = class_map[:, None] == jnp.arange(TILE, dtype=jnp.int32)[None, :]
    sums = lax.dot_general(
        member.astype(BF16), entity_feats, (((0,), (0,)), ((), ())), preferred_element_type=F32
    )
    counts = jnp.sum(member.astype(F32), axis=0)
    class_feat = (sums / counts[:, None]).astype(BF16)

    rels = jnp.pad(tile_rels, (0, 8), constant_values=-1)
    pick_rel = (rels[:, None] == jnp.arange(RELS, dtype=jnp.int32)[None, :]).astype(BF16)
    coef = jnp.dot(pick_rel, coefficients, preferred_element_type=F32)
    other = (tile_column_index % 2 != mine).astype(jnp.int32) * SLOTS
    ty = tile_column_index // (2 * NZ)
    tz = (tile_column_index // 2) % NZ
    xslot = other + tz * NY + ty
    dslot = other + ty * NZ + tz
    stacked = bases.reshape(B * H, H)

    with jax.named_scope("feats_y"):
        feats_y = spread_to(class_feat, "y", NY).reshape(NY * TILE, H)
    cotangent, feats_y = after(cotangent, feats_y)
    with jax.named_scope("feats_z"):
        feats_mine = lax.all_gather(feats_y, "z", axis=0, tiled=True)
    with jax.named_scope("cot_x"):
        cot_rows = lax.all_gather(cotangent, "x", axis=0, tiled=True)

    grads, keep, give = backward(
        tile_rows, dslot, tile_counts, coef, cot_rows, stacked, tile_values
    )
    with jax.named_scope("dx_c"):
        got = swap(give)
    dx = (keep.astype(F32) + got.astype(F32)).astype(BF16).reshape(NY * NZ * TILE, H)
    with jax.named_scope("dx_y"):
        dx = lax.psum_scatter(dx, "y", scatter_dimension=0, tiled=True)

    feats_mine = feats_mine.reshape(SLOTS, TILE, H)
    with jax.named_scope("feats_c"):
        feats_other = swap(feats_mine)
    rels = jnp.repeat(tile_rels, B)
    outp, dkeep, dgive, coefg = forward(
        tile_rows, xslot, tile_counts, mine[None], coef, rels[:, None], rels[None, :],
        feats_mine, feats_other, tile_values, grads, stacked, cot_rows,
    )

    with jax.named_scope("dv_c"):
        dgot = swap(dgive)
    dv = (dkeep + dgot[:1024].astype(F32)).reshape(NX, 256, H).astype(BF16)
    cg = coefg + dgot[1024:, :128].astype(F32) + dgot[1024:, 128:].astype(F32)
    cg_x = jnp.broadcast_to(two_parts(cg)[None], (NX, 32, H))
    with jax.named_scope("dv_x"):
        got_x = exchange(jnp.concatenate([dv, outp.reshape(NX, TILE, H), cg_x], axis=1), "x")
    got_x, dx = after(got_x, dx)
    with jax.named_scope("dx_z"):
        dx = lax.psum_scatter(dx.astype(F32), "z", scatter_dimension=0, tiled=True)
    sum_x = jnp.sum(got_x.astype(F32), axis=0)
    layer_out = sum_x[256:384].astype(BF16)
    cg = sum_x[384:, :128] + sum_x[384:, 128:]
    pad = jnp.zeros((NY * NZ, 7, H), BF16)
    packed = jnp.concatenate(
        [sum_x[:256].reshape(NY * NZ, 8, H).astype(BF16), two_parts(cg)[:, None, :], pad], axis=1
    )
    with jax.named_scope("dv_yz"):
        got_yz = exchange(packed, ("y", "z"))
    sum_yz = jnp.sum(got_yz.astype(F32), axis=0)
    cg = sum_yz[8:9, :128] + sum_yz[8:9, 128:]
    packed = jnp.concatenate(
        [sum_yz[:8].astype(BF16), two_parts(cg), jnp.zeros((7, H), BF16)], axis=0
    )
    with jax.named_scope("all_yz"):
        all_yz = spread_to(packed, ("y", "z"), NY * NZ)
    scale = (NY * NZ * NC * NX * TILE) ** (-0.5)
    cg = all_yz[:, 8, :128].astype(F32) + all_yz[:, 8, 128:].astype(F32)
    grad_coef = (cg * scale).reshape(512, B)[:RELS]
    with jax.named_scope("all_x"):
        all_x = spread_to(all_yz[:, :8].reshape(256, H), "x", NX).reshape(1024, H)
    all_x, dx = after(all_x, dx)
    with jax.named_scope("all_c"):
        all_other = swap(all_x)
    first = jnp.where(mine == 0, all_x, all_other)
    second = jnp.where(mine == 0, all_other, all_x)
    grad_bases = (jnp.stack([first, second]).astype(F32) * scale).reshape(B, H, H)

    quotient = dx / counts[:, None]
    grad_entities = jnp.dot(member.astype(F32), quotient, precision=lax.Precision.HIGHEST)
    return (layer_out, grad_entities, grad_bases, grad_coef)


def solution(mesh):
    grid = Mesh(mesh.devices.reshape(NY, NZ, NC, NX), DEVICES)
    by_tile = P(DEVICES)
    by_class = P(("x",) + ROWS)
    placed = (
        by_class,
        by_class,
        by_tile,
        by_tile,
        by_tile,
        by_tile,
        by_tile,
        P(),
        P(),
        by_tile,
    )
    return jax.shard_map(
        local,
        mesh=grid,
        in_specs=placed,
        out_specs=(by_tile, by_class, P(), P()),
        check_vma=False,
    )
```

```python
import jax
import jax.numpy as jnp
from jax import lax
from jax.experimental import pallas as pl
from jax.experimental.pallas import tpu as pltpu
from jax.sharding import Mesh
from jax.sharding import PartitionSpec as P

NY, NZ, NC, NX = 4, 8, 2, 4
TILE = 128
H = 256
B = 8
SLOTS = 32
TROWS = 4
RELS = 500
F32, BF16 = jnp.float32, jnp.bfloat16
ROWS = ("y", "z", "c")
DEVICES = ("y", "z", "c", "x")
VMEM = pl.BlockSpec(memory_space=pltpu.VMEM)
SMEM = pl.BlockSpec(memory_space=pltpu.SMEM)
ANY = pl.BlockSpec(memory_space=pl.ANY)
PARAMS = pltpu.CompilerParams(vmem_limit_bytes=32 * 2**20)


def far(x):
    return pltpu.with_memory_space_constraint(x, pltpu.HBM)


def near(x):
    return pltpu.with_memory_space_constraint(x, pltpu.VMEM)


def by_row(trow, count, order, filled):
    for t in range(TROWS):
        filled[t] = 0

    def put(s, carry):
        t = trow[s]
        n = filled[t]
        order[t, n] = s
        filled[t] = n + 1
        return carry

    lax.fori_loop(0, count[0], put, 0)
    for t in range(TROWS):
        order[t, filled[t]] = SLOTS


def pairs(order, filled, body):
    def row(t, carry):
        def pair(p, inner):
            body(t, order[t, 2 * p], order[t, 2 * p + 1])
            return inner

        lax.fori_loop(0, (filled[t] + 1) // 2, pair, 0)
        return carry

    lax.fori_loop(0, TROWS, row, 0)


def fold(x):
    return (x[:8, :128] + x[:8, 128:]) + (x[8:, :128] + x[8:, 128:])


def fours(count, body):
    def group(q, carry):
        for k in range(4):
            body(4 * q + k)
        return carry

    lax.fori_loop(0, (count[0] + 3) // 4, group, 0)


def backward_kernel(
    trow, dslot, count, coef, cot, bases, tiles, grads_out, keep, give,
    grads, wide, total, mixed, order, filled, sem,
):
    total[...] = jnp.zeros_like(total)
    mixed[...] = jnp.zeros_like(mixed)
    by_row(trow, count, order, filled)
    for b in range(B):
        g = lax.dot_general(
            cot[...], bases[pl.ds(b * H, H), :], (((1,), (1,)), ((), ())), preferred_element_type=F32
        ).astype(BF16)
        grads[:, b] = g.reshape(TROWS, TILE, H)
        wide[:, b] = g.astype(F32).reshape(TROWS, TILE, H)
    store = pltpu.make_async_copy(grads, grads_out, sem)
    store.start()

    def mix(t, s1, s2):
        c1 = [coef[s1, b] for b in range(B)]
        c2 = [coef[s2, b] for b in range(B)]
        for r in range(4):
            rows = pl.ds(r * 32, 32)
            g = wide[t, 0, rows, :]
            m1 = c1[0] * g
            m2 = c2[0] * g
            for b in range(1, B):
                g = wide[t, b, rows, :]
                m1 = m1 + c1[b] * g
                m2 = m2 + c2[b] * g
            mixed[s1, rows, :] = m1.astype(BF16)
            mixed[s2, rows, :] = m2.astype(BF16)

    pairs(order, filled, mix)

    def back(s):
        d = dslot[s]
        total[d] = total[d] + lax.dot_general(
            tiles[s], mixed[s], (((0,), (0,)), ((), ())), preferred_element_type=F32
        )

    fours(count, back)
    keep[...] = total[pl.ds(0, SLOTS)].astype(BF16)
    give[...] = total[pl.ds(SLOTS, SLOTS)].astype(BF16)
    store.wait()


def backward(trow, dslot, count, coef, cot_rows, stacked, tile_values):
    blocks = pltpu.VMEM((SLOTS, TILE, H), BF16)
    return pl.pallas_call(
        backward_kernel,
        in_specs=[SMEM] * 4 + [VMEM] * 3,
        out_specs=[ANY] + [VMEM] * 2,
        out_shape=[pltpu.HBM((TROWS, B, TILE, H), BF16), blocks, blocks],
        scratch_shapes=[
            pltpu.VMEM((TROWS, B, TILE, H), BF16),
            pltpu.VMEM((TROWS, B, TILE, H), F32),
            pltpu.VMEM((2 * SLOTS, TILE, H), F32),
            pltpu.VMEM((SLOTS + 1, TILE, H), BF16),
            pltpu.SMEM((TROWS, SLOTS + 8), jnp.int32),
            pltpu.SMEM((TROWS,), jnp.int32),
            pltpu.SemaphoreType.DMA(()),
        ],
        compiler_params=PARAMS,
        name="backward",
    )(trow, dslot, count, coef, *map(near, (cot_rows, stacked, tile_values)))


def forward_kernel(
    trow, xslot, count, half, coef, relc, relr, xmine, xother, tiles_in, grads_in, bases_in, cot,
    outp, dkeep, dgive, coefg,
    feats, tiles, grads, bases, sums, part, msg, gram, order, filled, sems,
):
    loads = [
        pltpu.make_async_copy(src, dst, sems.at[k])
        for k, (src, dst) in enumerate(
            (
                (xmine, feats.at[pl.ds(0, SLOTS)]),
                (xother, feats.at[pl.ds(SLOTS, SLOTS)]),
                (tiles_in, tiles),
                (grads_in, grads),
                (bases_in, bases),
            )
        )
    ]
    for copy in loads:
        copy.start()
    sums[...] = jnp.zeros_like(sums)
    msg[SLOTS] = jnp.zeros((TILE, H), F32)
    gram[...] = jnp.zeros_like(gram)
    by_row(trow, count, order, filled)
    for copy in loads[:3]:
        copy.wait()

    def message(s):
        m = jnp.dot(tiles[s], feats[xslot[s]], preferred_element_type=F32).astype(BF16)
        msg[s] = m.astype(F32)

    fours(count, message)
    loads[3].wait()

    def add(t, s1, s2):
        c1 = [coef[s1, b] for b in range(B)]
        c2 = [coef[s2, b] for b in range(B)]
        d1 = [jnp.zeros((8, 128), F32)] * B
        d2 = [jnp.zeros((8, 128), F32)] * B
        for r in range(8):
            rows = pl.ds(r * 16, 16)
            m1 = msg[s1, rows, :]
            m2 = msg[s2, rows, :]
            for b in range(B):
                sums[t, b, rows, :] = sums[t, b, rows, :] + (c1[b] * m1 + c2[b] * m2)
                g = grads[t, b, rows, :].astype(F32)
                d1[b] = d1[b] + fold(m1 * g)
                d2[b] = d2[b] + fold(m2 * g)
        for b in range(B):
            gram[s1, b] = d1[b]
            gram[s2, b] = d2[b]

    pairs(order, filled, add)

    for t in range(TROWS):
        for b in range(B):
            part[pl.ds(t * TILE, TILE), pl.ds(b * H, H)] = sums[t, b].astype(BF16)
    loads[4].wait()
    outp[...] = jnp.dot(part[...], bases[...], preferred_element_type=F32).astype(BF16)
    mine = half[0]

    def outer(k):
        cols = pl.ds(pl.multiple_of(k * H, H), H)
        return lax.dot_general(
            part[:, cols], cot[...], (((0,), (0,)), ((), ())), preferred_element_type=F32
        )

    for k in range(B // 2):
        rows = pl.ds(k * H, H)
        dkeep[rows, :] = outer(mine * (B // 2) + k)
        dgive[rows, :] = outer((1 - mine) * (B // 2) + k).astype(BF16)

    col = jnp.sum(jnp.sum(gram[pl.ds(0, SLOTS)].reshape(SLOTS * B, 8, 128), axis=1), axis=1, keepdims=True)
    lane = lax.broadcasted_iota(jnp.int32, (SLOTS * B, 128), 1)
    row = lax.broadcasted_iota(jnp.int32, (SLOTS * B, 128), 0)
    pick = (lane % B == row % B) & (lane // B == relc[...] % 16) & (row < count[0] * B)
    spread = jnp.where(pick, col, 0.0)
    line = lax.broadcasted_iota(jnp.int32, (32, SLOTS * B), 0)
    gather = (relr[...] // 16 == line).astype(F32)
    cg = jnp.dot(gather, spread, precision=lax.Precision.HIGHEST, preferred_element_type=F32)
    coefg[...] = cg
    hi = cg.astype(BF16)
    dgive[pl.ds(1024, 32), pl.ds(0, 128)] = hi
    dgive[pl.ds(1024, 32), pl.ds(128, 128)] = (cg - hi.astype(F32)).astype(BF16)


def forward(trow, xslot, count, half, coef, relc, relr, xmine, xother, tiles, grads, stacked, cot_rows):
    return pl.pallas_call(
        forward_kernel,
        in_specs=[SMEM] * 5 + [VMEM] * 2 + [ANY] * 5 + [VMEM],
        out_specs=[VMEM] * 4,
        out_shape=[
            pltpu.VMEM((TROWS * TILE, H), BF16),
            pltpu.VMEM((1024, H), F32),
            pltpu.VMEM((1056, H), BF16),
            pltpu.VMEM((32, 128), F32),
        ],
        scratch_shapes=[
            pltpu.VMEM((2 * SLOTS, TILE, H), BF16),
            pltpu.VMEM((SLOTS, TILE, TILE), BF16),
            pltpu.VMEM((TROWS, B, TILE, H), BF16),
            pltpu.VMEM((B * H, H), BF16),
            pltpu.VMEM((TROWS, B, TILE, H), F32),
            pltpu.VMEM((TROWS * TILE, B * H), BF16),
            pltpu.VMEM((SLOTS + 1, TILE, H), F32),
            pltpu.VMEM((SLOTS + 1, B, 8, 128), F32),
            pltpu.SMEM((TROWS, SLOTS + 8), jnp.int32),
            pltpu.SMEM((TROWS,), jnp.int32),
            pltpu.SemaphoreType.DMA((5,)),
        ],
        compiler_params=PARAMS,
        name="forward",
    )(
        trow, xslot, count, half, coef, relc, relr,
        *map(far, (xmine, xother, tiles, grads, stacked)), near(cot_rows),
    )


def swap(x):
    return lax.ppermute(x, "c", [(0, 1), (1, 0)])


def exchange(x, axes):
    return lax.all_to_all(x, axes, split_axis=0, concat_axis=0, tiled=True)


def spread_to(x, axes, n):
    return exchange(jnp.broadcast_to(x[None], (n,) + x.shape), axes)


def two_parts(x):
    hi = lax.reduce_precision(x, 8, 7)
    return jnp.concatenate([hi, x - hi], axis=-1).astype(BF16)


def after(x, y):
    return lax.optimization_barrier((x, y))


def local(
    entity_feats,
    class_map,
    tile_values,
    tile_rows,
    tile_column_index,
    tile_rels,
    tile_counts,
    coefficients,
    bases,
    cotangent,
):
    mine = lax.axis_index("c").astype(jnp.int32)
    member = class_map[:, None] == jnp.arange(TILE, dtype=jnp.int32)[None, :]
    sums = lax.dot_general(
        member.astype(BF16), entity_feats, (((0,), (0,)), ((), ())), preferred_element_type=F32
    )
    counts = jnp.sum(member.astype(F32), axis=0)
    class_feat = (sums / counts[:, None]).astype(BF16)

    rels = jnp.pad(tile_rels, (0, 8), constant_values=-1)
    pick_rel = (rels[:, None] == jnp.arange(RELS, dtype=jnp.int32)[None, :]).astype(BF16)
    coef = jnp.dot(pick_rel, coefficients, preferred_element_type=F32)
    other = (tile_column_index % 2 != mine).astype(jnp.int32) * SLOTS
    ty = tile_column_index // (2 * NZ)
    tz = (tile_column_index // 2) % NZ
    xslot = other + tz * NY + ty
    dslot = other + ty * NZ + tz
    stacked = bases.reshape(B * H, H)

    with jax.named_scope("feats_y"):
        feats_y = spread_to(class_feat, "y", NY).reshape(NY * TILE, H)
    cotangent, feats_y = after(cotangent, feats_y)
    with jax.named_scope("feats_z"):
        feats_mine = lax.all_gather(feats_y, "z", axis=0, tiled=True)
    with jax.named_scope("cot_x"):
        cot_rows = lax.all_gather(cotangent, "x", axis=0, tiled=True)

    grads, keep, give = backward(
        tile_rows, dslot, tile_counts, coef, cot_rows, stacked, tile_values
    )
    with jax.named_scope("dx_c"):
        got = swap(give)
    dx = (keep.astype(F32) + got.astype(F32)).astype(BF16).reshape(NY * NZ * TILE, H)
    with jax.named_scope("dx_y"):
        dx = lax.psum_scatter(dx, "y", scatter_dimension=0, tiled=True)

    feats_mine = feats_mine.reshape(SLOTS, TILE, H)
    with jax.named_scope("feats_c"):
        feats_other = swap(feats_mine)
    rels = jnp.repeat(tile_rels, B)
    outp, dkeep, dgive, coefg = forward(
        tile_rows, xslot, tile_counts, mine[None], coef, rels[:, None], rels[None, :],
        feats_mine, feats_other, tile_values, grads, stacked, cot_rows,
    )

    with jax.named_scope("dv_c"):
        dgot = swap(dgive)
    dv = (dkeep + dgot[:1024].astype(F32)).reshape(NX, 256, H).astype(BF16)
    cg = coefg + dgot[1024:, :128].astype(F32) + dgot[1024:, 128:].astype(F32)
    cg_x = jnp.broadcast_to(two_parts(cg)[None], (NX, 32, H))
    send_x = jnp.concatenate([dv, outp.reshape(NX, TILE, H), cg_x], axis=1)
    send_x, dx = after(send_x, dx)
    with jax.named_scope("dx_z"):
        dx = lax.psum_scatter(dx.astype(F32), "z", scatter_dimension=0, tiled=True)
    with jax.named_scope("dv_x"):
        got_x = exchange(send_x, "x")
    sum_x = jnp.sum(got_x.astype(F32), axis=0)
    layer_out = sum_x[256:384].astype(BF16)
    cg = sum_x[384:, :128] + sum_x[384:, 128:]
    pad = jnp.zeros((NY * NZ, 7, H), BF16)
    packed = jnp.concatenate(
        [sum_x[:256].reshape(NY * NZ, 8, H).astype(BF16), two_parts(cg)[:, None, :], pad], axis=1
    )
    with jax.named_scope("dv_yz"):
        got_yz = exchange(packed, ("y", "z"))
    sum_yz = jnp.sum(got_yz.astype(F32), axis=0)
    cg = sum_yz[8:9, :128] + sum_yz[8:9, 128:]
    packed = jnp.concatenate(
        [sum_yz[:8].astype(BF16), two_parts(cg), jnp.zeros((7, H), BF16)], axis=0
    )
    with jax.named_scope("all_yz"):
        all_yz = spread_to(packed, ("y", "z"), NY * NZ)
    scale = (NY * NZ * NC * NX * TILE) ** (-0.5)
    cg = all_yz[:, 8, :128].astype(F32) + all_yz[:, 8, 128:].astype(F32)
    grad_coef = (cg * scale).reshape(512, B)[:RELS]
    all_yz, dx = after(all_yz, dx)
    with jax.named_scope("all_x"):
        all_x = spread_to(all_yz[:, :8].reshape(256, H), "x", NX).reshape(1024, H)
    with jax.named_scope("all_c"):
        all_other = swap(all_x)
    first = jnp.where(mine == 0, all_x, all_other)
    second = jnp.where(mine == 0, all_other, all_x)
    grad_bases = (jnp.stack([first, second]).astype(F32) * scale).reshape(B, H, H)

    quotient = dx / counts[:, None]
    grad_entities = jnp.dot(member.astype(F32), quotient, precision=lax.Precision.HIGHEST)
    return (layer_out, grad_entities, grad_bases, grad_coef)


def solution(mesh):
    grid = Mesh(mesh.devices.reshape(NY, NZ, NC, NX), DEVICES)
    by_tile = P(DEVICES)
    by_class = P(("x",) + ROWS)
    placed = (
        by_class,
        by_class,
        by_tile,
        by_tile,
        by_tile,
        by_tile,
        by_tile,
        P(),
        P(),
        by_tile,
    )
    return jax.shard_map(
        local,
        mesh=grid,
        in_specs=placed,
        out_specs=(by_tile, by_class, P(), P()),
        check_vma=False,
    )
```

```python
import jax
import jax.numpy as jnp
from jax import lax
from jax.experimental import pallas as pl
from jax.experimental.pallas import tpu as pltpu
from jax.sharding import Mesh
from jax.sharding import PartitionSpec as P

NY, NZ, NC, NX = 4, 8, 2, 4
TILE = 128
H = 256
B = 8
SLOTS = 32
TROWS = 4
RELS = 500
F32, BF16 = jnp.float32, jnp.bfloat16
ROWS = ("y", "z", "c")
DEVICES = ("y", "z", "c", "x")
VMEM = pl.BlockSpec(memory_space=pltpu.VMEM)
SMEM = pl.BlockSpec(memory_space=pltpu.SMEM)
ANY = pl.BlockSpec(memory_space=pl.ANY)
PARAMS = pltpu.CompilerParams(vmem_limit_bytes=24 * 2**20)


def far(x):
    return pltpu.with_memory_space_constraint(x, pltpu.HBM)


def near(x):
    return pltpu.with_memory_space_constraint(x, pltpu.VMEM)


def by_row(trow, count, order, filled):
    for t in range(TROWS):
        filled[t] = 0

    def put(s, carry):
        t = trow[s]
        n = filled[t]
        order[t, n] = s
        filled[t] = n + 1
        return carry

    lax.fori_loop(0, count[0], put, 0)
    for t in range(TROWS):
        order[t, filled[t]] = SLOTS


def pairs(order, filled, body):
    def row(t, carry):
        def pair(p, inner):
            body(t, order[t, 2 * p], order[t, 2 * p + 1])
            return inner

        lax.fori_loop(0, (filled[t] + 1) // 2, pair, 0)
        return carry

    lax.fori_loop(0, TROWS, row, 0)


def fold(x):
    return (x[:8, :128] + x[:8, 128:]) + (x[8:, :128] + x[8:, 128:])


def fours(count, body):
    def group(q, carry):
        for k in range(4):
            body(4 * q + k)
        return carry

    lax.fori_loop(0, (count[0] + 3) // 4, group, 0)


def backward_kernel(
    trow, dslot, count, coef, cot, bases, tiles, grads_out, keep, give,
    grads, wide, total, mixed, order, filled, sem,
):
    total[...] = jnp.zeros_like(total)
    mixed[...] = jnp.zeros_like(mixed)
    by_row(trow, count, order, filled)
    for b in range(B):
        g = lax.dot_general(
            cot[...], bases[pl.ds(b * H, H), :], (((1,), (1,)), ((), ())), preferred_element_type=F32
        ).astype(BF16)
        grads[:, b] = g.reshape(TROWS, TILE, H)
        wide[:, b] = g.astype(F32).reshape(TROWS, TILE, H)
    store = pltpu.make_async_copy(grads, grads_out, sem)
    store.start()

    def mix(t, s1, s2):
        c1 = [coef[s1, b] for b in range(B)]
        c2 = [coef[s2, b] for b in range(B)]
        for r in range(4):
            rows = pl.ds(r * 32, 32)
            g = wide[t, 0, rows, :]
            m1 = c1[0] * g
            m2 = c2[0] * g
            for b in range(1, B):
                g = wide[t, b, rows, :]
                m1 = m1 + c1[b] * g
                m2 = m2 + c2[b] * g
            mixed[s1, rows, :] = m1.astype(BF16)
            mixed[s2, rows, :] = m2.astype(BF16)

    pairs(order, filled, mix)

    def back(s):
        d = dslot[s]
        total[d] = total[d] + lax.dot_general(
            tiles[s], mixed[s], (((0,), (0,)), ((), ())), preferred_element_type=F32
        )

    fours(count, back)
    keep[...] = total[pl.ds(0, SLOTS)].astype(BF16)
    give[...] = total[pl.ds(SLOTS, SLOTS)].astype(BF16)
    store.wait()


def backward(trow, dslot, count, coef, cot_rows, stacked, tile_values):
    blocks = pltpu.VMEM((SLOTS, TILE, H), BF16)
    return pl.pallas_call(
        backward_kernel,
        in_specs=[SMEM] * 4 + [VMEM] * 3,
        out_specs=[ANY] + [VMEM] * 2,
        out_shape=[pltpu.HBM((TROWS, B, TILE, H), BF16), blocks, blocks],
        scratch_shapes=[
            pltpu.VMEM((TROWS, B, TILE, H), BF16),
            pltpu.VMEM((TROWS, B, TILE, H), F32),
            pltpu.VMEM((2 * SLOTS, TILE, H), F32),
            pltpu.VMEM((SLOTS + 1, TILE, H), BF16),
            pltpu.SMEM((TROWS, SLOTS + 8), jnp.int32),
            pltpu.SMEM((TROWS,), jnp.int32),
            pltpu.SemaphoreType.DMA(()),
        ],
        compiler_params=PARAMS,
        name="backward",
    )(trow, dslot, count, coef, *map(near, (cot_rows, stacked, tile_values)))


def forward_kernel(
    trow, xslot, count, half, coef, xmine, xother, tiles, bases, cot,
    outp, dkeep, dgive, sent,
    feats, sums, part, msg, short, order, filled, sems,
):
    loads = [
        pltpu.make_async_copy(src, dst, sems.at[k])
        for k, (src, dst) in enumerate(
            (
                (xmine, feats.at[pl.ds(0, SLOTS)]),
                (xother, feats.at[pl.ds(SLOTS, SLOTS)]),
            )
        )
    ]
    for copy in loads:
        copy.start()
    sums[...] = jnp.zeros_like(sums)
    msg[SLOTS] = jnp.zeros((TILE, H), F32)
    short[...] = jnp.zeros_like(short)
    by_row(trow, count, order, filled)
    for copy in loads:
        copy.wait()

    def message(s):
        m = jnp.dot(tiles[s], feats[xslot[s]], preferred_element_type=F32).astype(BF16)
        short[s] = m
        msg[s] = m.astype(F32)

    fours(count, message)
    store = pltpu.make_async_copy(short, sent, sems.at[2])
    store.start()

    def add(t, s1, s2):
        c1 = [coef[s1, b] for b in range(B)]
        c2 = [coef[s2, b] for b in range(B)]
        for r in range(8):
            rows = pl.ds(r * 16, 16)
            m1 = msg[s1, rows, :]
            m2 = msg[s2, rows, :]
            for b in range(B):
                sums[t, b, rows, :] = sums[t, b, rows, :] + (c1[b] * m1 + c2[b] * m2)

    pairs(order, filled, add)

    for t in range(TROWS):
        for b in range(B):
            part[pl.ds(t * TILE, TILE), pl.ds(b * H, H)] = sums[t, b].astype(BF16)
    outp[...] = jnp.dot(part[...], bases[...], preferred_element_type=F32).astype(BF16)
    mine = half[0]

    def outer(k):
        cols = pl.ds(pl.multiple_of(k * H, H), H)
        return lax.dot_general(
            part[:, cols], cot[...], (((0,), (0,)), ((), ())), preferred_element_type=F32
        )

    for k in range(B // 2):
        rows = pl.ds(k * H, H)
        dkeep[rows, :] = outer(mine * (B // 2) + k)
        dgive[rows, :] = outer((1 - mine) * (B // 2) + k).astype(BF16)
    store.wait()


def forward(trow, xslot, count, half, coef, xmine, xother, tiles, stacked, cot_rows):
    return pl.pallas_call(
        forward_kernel,
        in_specs=[SMEM] * 5 + [ANY] * 2 + [VMEM] * 3,
        out_specs=[VMEM] * 3 + [ANY],
        out_shape=[
            pltpu.VMEM((TROWS * TILE, H), BF16),
            pltpu.VMEM((1024, H), F32),
            pltpu.VMEM((1024, H), BF16),
            pltpu.HBM((SLOTS, TILE, H), BF16),
        ],
        scratch_shapes=[
            pltpu.VMEM((2 * SLOTS, TILE, H), BF16),
            pltpu.VMEM((TROWS, B, TILE, H), F32),
            pltpu.VMEM((TROWS * TILE, B * H), BF16),
            pltpu.VMEM((SLOTS + 1, TILE, H), F32),
            pltpu.VMEM((SLOTS, TILE, H), BF16),
            pltpu.SMEM((TROWS, SLOTS + 8), jnp.int32),
            pltpu.SMEM((TROWS,), jnp.int32),
            pltpu.SemaphoreType.DMA((3,)),
        ],
        compiler_params=PARAMS,
        name="forward",
    )(
        trow, xslot, count, half, coef,
        *map(far, (xmine, xother)), *map(near, (tiles, stacked, cot_rows)),
    )


def gram_kernel(
    trow, count, relc, relr, sent, grads_in, coefg, msg, grads, gram, order, filled, sems
):
    loads = [
        pltpu.make_async_copy(sent, msg.at[pl.ds(0, SLOTS)], sems.at[0]),
        pltpu.make_async_copy(grads_in, grads, sems.at[1]),
    ]
    for copy in loads:
        copy.start()
    msg[SLOTS] = jnp.zeros((TILE, H), BF16)
    gram[...] = jnp.zeros_like(gram)
    by_row(trow, count, order, filled)
    for copy in loads:
        copy.wait()

    def dots(t, s1, s2):
        d1 = [jnp.zeros((8, 128), F32)] * B
        d2 = [jnp.zeros((8, 128), F32)] * B
        for r in range(8):
            rows = pl.ds(r * 16, 16)
            m1 = msg[s1, rows, :].astype(F32)
            m2 = msg[s2, rows, :].astype(F32)
            for b in range(B):
                g = grads[t, b, rows, :].astype(F32)
                d1[b] = d1[b] + fold(m1 * g)
                d2[b] = d2[b] + fold(m2 * g)
        for b in range(B):
            gram[s1, b] = d1[b]
            gram[s2, b] = d2[b]

    pairs(order, filled, dots)
    col = jnp.sum(jnp.sum(gram[pl.ds(0, SLOTS)].reshape(SLOTS * B, 8, 128), axis=1), axis=1, keepdims=True)
    lane = lax.broadcasted_iota(jnp.int32, (SLOTS * B, 128), 1)
    row = lax.broadcasted_iota(jnp.int32, (SLOTS * B, 128), 0)
    pick = (lane % B == row % B) & (lane // B == relc[...] % 16) & (row < count[0] * B)
    spread = jnp.where(pick, col, 0.0)
    line = lax.broadcasted_iota(jnp.int32, (32, SLOTS * B), 0)
    gather = (relr[...] // 16 == line).astype(F32)
    cg = jnp.dot(gather, spread, precision=lax.Precision.HIGHEST, preferred_element_type=F32)
    coefg[...] = cg


def gram_sums(trow, count, relc, relr, sent, grads):
    return pl.pallas_call(
        gram_kernel,
        in_specs=[SMEM] * 2 + [VMEM] * 2 + [ANY] * 2,
        out_specs=VMEM,
        out_shape=jax.ShapeDtypeStruct((32, 128), F32),
        scratch_shapes=[
            pltpu.VMEM((SLOTS + 1, TILE, H), BF16),
            pltpu.VMEM((TROWS, B, TILE, H), BF16),
            pltpu.VMEM((SLOTS + 1, B, 8, 128), F32),
            pltpu.SMEM((TROWS, SLOTS + 8), jnp.int32),
            pltpu.SMEM((TROWS,), jnp.int32),
            pltpu.SemaphoreType.DMA((2,)),
        ],
        compiler_params=PARAMS,
        name="gram",
    )(trow, count, relc, relr, far(sent), far(grads))


def swap(x):
    return lax.ppermute(x, "c", [(0, 1), (1, 0)])


def exchange(x, axes):
    return lax.all_to_all(x, axes, split_axis=0, concat_axis=0, tiled=True)


def spread_to(x, axes, n):
    return exchange(jnp.broadcast_to(x[None], (n,) + x.shape), axes)


def two_parts(x):
    hi = lax.reduce_precision(x, 8, 7)
    return jnp.concatenate([hi, x - hi], axis=-1).astype(BF16)


def one_part(x):
    return x[..., :128] + x[..., 128:]


def after(x, y):
    return lax.optimization_barrier((x, y))


def local(
    entity_feats,
    class_map,
    tile_values,
    tile_rows,
    tile_column_index,
    tile_rels,
    tile_counts,
    coefficients,
    bases,
    cotangent,
):
    mine = lax.axis_index("c").astype(jnp.int32)
    member = class_map[:, None] == jnp.arange(TILE, dtype=jnp.int32)[None, :]
    sums = lax.dot_general(
        member.astype(BF16), entity_feats, (((0,), (0,)), ((), ())), preferred_element_type=F32
    )
    counts = jnp.sum(member.astype(F32), axis=0)
    class_feat = (sums / counts[:, None]).astype(BF16)

    rels = jnp.pad(tile_rels, (0, 8), constant_values=-1)
    pick_rel = (rels[:, None] == jnp.arange(RELS, dtype=jnp.int32)[None, :]).astype(BF16)
    coef = jnp.dot(pick_rel, coefficients, preferred_element_type=F32)
    other = (tile_column_index % 2 != mine).astype(jnp.int32) * SLOTS
    ty = tile_column_index // (2 * NZ)
    tz = (tile_column_index // 2) % NZ
    xslot = other + tz * NY + ty
    dslot = other + ty * NZ + tz
    stacked = bases.reshape(B * H, H)

    with jax.named_scope("feats_y"):
        feats_y = spread_to(class_feat, "y", NY).reshape(NY * TILE, H)
    cotangent, feats_y = after(cotangent, feats_y)
    with jax.named_scope("feats_z"):
        feats_mine = lax.all_gather(feats_y, "z", axis=0, tiled=True)
    with jax.named_scope("cot_x"):
        cot_rows = lax.all_gather(cotangent, "x", axis=0, tiled=True)

    grads, keep, give = backward(
        tile_rows, dslot, tile_counts, coef, cot_rows, stacked, tile_values
    )
    with jax.named_scope("dx_c"):
        got = swap(give)
    dx = (keep.astype(F32) + got.astype(F32)).astype(BF16).reshape(NY * NZ * TILE, H)
    with jax.named_scope("dx_y"):
        dx = lax.psum_scatter(dx, "y", scatter_dimension=0, tiled=True)

    feats_mine = feats_mine.reshape(SLOTS, TILE, H)
    with jax.named_scope("feats_c"):
        feats_other = swap(feats_mine)
    rels = jnp.repeat(tile_rels, B)
    outp, dkeep, dgive, sent = forward(
        tile_rows, xslot, tile_counts, mine[None], coef,
        feats_mine, feats_other, tile_values, stacked, cot_rows,
    )

    with jax.named_scope("dv_c"):
        dgot = swap(dgive)
    dv = (dkeep + dgot.astype(F32)).reshape(NX, 256, H).astype(BF16)
    send_x = jnp.concatenate([dv, outp.reshape(NX, TILE, H)], axis=1)
    send_x, dx = after(send_x, dx)
    sent, dx = after(sent, dx.astype(F32))
    with jax.named_scope("dx_z"):
        dx = lax.psum_scatter(dx, "z", scatter_dimension=0, tiled=True)
    with jax.named_scope("dv_x"):
        got_x = exchange(send_x, "x")
    cg = gram_sums(tile_rows, tile_counts, rels[:, None], rels[None, :], sent, grads)
    (sum_x,) = lax.optimization_barrier((jnp.sum(got_x.astype(F32), axis=0),))
    layer_out = sum_x[256:].astype(BF16)
    pad = jnp.zeros((NY * NZ, 7, H), BF16)
    packed = jnp.concatenate(
        [sum_x[:256].reshape(NY * NZ, 8, H).astype(BF16), two_parts(cg)[:, None, :], pad], axis=1
    )
    with jax.named_scope("dv_yz"):
        got_yz = exchange(packed, ("y", "z"))
    sum_yz = jnp.sum(got_yz.astype(F32), axis=0)
    packed = jnp.concatenate(
        [sum_yz[:8].astype(BF16), two_parts(one_part(sum_yz[8:9])), jnp.zeros((7, H), BF16)], axis=0
    )
    with jax.named_scope("all_yz"):
        all_yz = spread_to(packed, ("y", "z"), NY * NZ)
    all_yz, dx = after(all_yz, dx)
    send_x = jnp.concatenate([all_yz[:, :8].reshape(256, H), all_yz[:, 8]], axis=0)
    with jax.named_scope("all_x"):
        all_x = spread_to(send_x, "x", NX)
    cg = two_parts(jnp.sum(one_part(all_x[:, 256:].astype(F32)), axis=0))
    send_c = jnp.concatenate([all_x[:, :256].reshape(1024, H), cg], axis=0)
    with jax.named_scope("all_c"):
        got_c = swap(send_c)
    scale = (NY * NZ * NC * NX * TILE) ** (-0.5)
    cg = one_part(send_c[1024:].astype(F32)) + one_part(got_c[1024:].astype(F32))
    grad_coef = (cg * scale).reshape(512, B)[:RELS]
    first = jnp.where(mine == 0, send_c[:1024], got_c[:1024])
    second = jnp.where(mine == 0, got_c[:1024], send_c[:1024])
    grad_bases = (jnp.stack([first, second]).astype(F32) * scale).reshape(B, H, H)

    quotient = dx / counts[:, None]
    grad_entities = jnp.dot(member.astype(F32), quotient, precision=lax.Precision.HIGHEST)
    return (layer_out, grad_entities, grad_bases, grad_coef)


def solution(mesh):
    grid = Mesh(mesh.devices.reshape(NY, NZ, NC, NX), DEVICES)
    by_tile = P(DEVICES)
    by_class = P(("x",) + ROWS)
    placed = (
        by_class,
        by_class,
        by_tile,
        by_tile,
        by_tile,
        by_tile,
        by_tile,
        P(),
        P(),
        by_tile,
    )
    return jax.shard_map(
        local,
        mesh=grid,
        in_specs=placed,
        out_specs=(by_tile, by_class, P(), P()),
        check_vma=False,
    )
```

```python
import jax
import jax.numpy as jnp
from jax import lax
from jax.experimental import pallas as pl
from jax.experimental.pallas import tpu as pltpu
from jax.sharding import Mesh
from jax.sharding import PartitionSpec as P

NY, NZ, NC, NX = 4, 8, 2, 4
TILE = 128
H = 256
B = 8
SLOTS = 32
TROWS = 4
RELS = 500
F32, BF16 = jnp.float32, jnp.bfloat16
ROWS = ("y", "z", "c")
DEVICES = ("y", "z", "c", "x")
VMEM = pl.BlockSpec(memory_space=pltpu.VMEM)
SMEM = pl.BlockSpec(memory_space=pltpu.SMEM)
ANY = pl.BlockSpec(memory_space=pl.ANY)
PARAMS = pltpu.CompilerParams(vmem_limit_bytes=24 * 2**20)


def far(x):
    return pltpu.with_memory_space_constraint(x, pltpu.HBM)


def near(x):
    return pltpu.with_memory_space_constraint(x, pltpu.VMEM)


def by_row(trow, count, order, filled):
    for t in range(TROWS):
        filled[t] = 0

    def put(s, carry):
        t = trow[s]
        n = filled[t]
        order[t, n] = s
        filled[t] = n + 1
        return carry

    lax.fori_loop(0, count[0], put, 0)
    for t in range(TROWS):
        order[t, filled[t]] = SLOTS


def pairs(order, filled, body):
    def row(t, carry):
        def pair(p, inner):
            body(t, order[t, 2 * p], order[t, 2 * p + 1])
            return inner

        lax.fori_loop(0, (filled[t] + 1) // 2, pair, 0)
        return carry

    lax.fori_loop(0, TROWS, row, 0)


def fold(x):
    return (x[:8, :128] + x[:8, 128:]) + (x[8:, :128] + x[8:, 128:])


def fours(count, body):
    def group(q, carry):
        for k in range(4):
            body(4 * q + k)
        return carry

    lax.fori_loop(0, (count[0] + 3) // 4, group, 0)


def backward_kernel(
    trow, dslot, count, coef, cot, bases, tiles, grads_out, keep, give,
    grads, wide, total, mixed, order, filled, sem,
):
    total[...] = jnp.zeros_like(total)
    mixed[...] = jnp.zeros_like(mixed)
    by_row(trow, count, order, filled)
    for b in range(B):
        g = lax.dot_general(
            cot[...], bases[pl.ds(b * H, H), :], (((1,), (1,)), ((), ())), preferred_element_type=F32
        ).astype(BF16)
        grads[:, b] = g.reshape(TROWS, TILE, H)
        wide[:, b] = g.astype(F32).reshape(TROWS, TILE, H)
    store = pltpu.make_async_copy(grads, grads_out, sem)
    store.start()

    def mix(t, s1, s2):
        c1 = [coef[s1, b] for b in range(B)]
        c2 = [coef[s2, b] for b in range(B)]
        for r in range(4):
            rows = pl.ds(r * 32, 32)
            g = wide[t, 0, rows, :]
            m1 = c1[0] * g
            m2 = c2[0] * g
            for b in range(1, B):
                g = wide[t, b, rows, :]
                m1 = m1 + c1[b] * g
                m2 = m2 + c2[b] * g
            mixed[s1, rows, :] = m1.astype(BF16)
            mixed[s2, rows, :] = m2.astype(BF16)

    pairs(order, filled, mix)

    def back(s):
        d = dslot[s]
        total[d] = total[d] + lax.dot_general(
            tiles[s], mixed[s], (((0,), (0,)), ((), ())), preferred_element_type=F32
        )

    fours(count, back)
    keep[...] = total[pl.ds(0, SLOTS)].astype(BF16)
    give[...] = total[pl.ds(SLOTS, SLOTS)].astype(BF16)
    store.wait()


def backward(trow, dslot, count, coef, cot_rows, stacked, tile_values):
    blocks = pltpu.VMEM((SLOTS, TILE, H), BF16)
    return pl.pallas_call(
        backward_kernel,
        in_specs=[SMEM] * 4 + [VMEM] * 3,
        out_specs=[ANY] + [VMEM] * 2,
        out_shape=[pltpu.HBM((TROWS, B, TILE, H), BF16), blocks, blocks],
        scratch_shapes=[
            pltpu.VMEM((TROWS, B, TILE, H), BF16),
            pltpu.VMEM((TROWS, B, TILE, H), F32),
            pltpu.VMEM((2 * SLOTS, TILE, H), F32),
            pltpu.VMEM((SLOTS + 1, TILE, H), BF16),
            pltpu.SMEM((TROWS, SLOTS + 8), jnp.int32),
            pltpu.SMEM((TROWS,), jnp.int32),
            pltpu.SemaphoreType.DMA(()),
        ],
        compiler_params=PARAMS,
        name="backward",
    )(trow, dslot, count, coef, *map(near, (cot_rows, stacked, tile_values)))


def forward_kernel(
    trow, xslot, count, half, coef, xmine, xother, tiles, bases, cot,
    outp, dkeep, dgive, sent,
    feats, sums, part, msg, short, order, filled, sems,
):
    loads = [
        pltpu.make_async_copy(src, dst, sems.at[k])
        for k, (src, dst) in enumerate(
            (
                (xmine, feats.at[pl.ds(0, SLOTS)]),
                (xother, feats.at[pl.ds(SLOTS, SLOTS)]),
            )
        )
    ]
    for copy in loads:
        copy.start()
    sums[...] = jnp.zeros_like(sums)
    msg[SLOTS] = jnp.zeros((TILE, H), F32)
    short[...] = jnp.zeros_like(short)
    by_row(trow, count, order, filled)
    for copy in loads:
        copy.wait()

    def message(s):
        m = jnp.dot(tiles[s], feats[xslot[s]], preferred_element_type=F32).astype(BF16)
        short[s] = m
        msg[s] = m.astype(F32)

    fours(count, message)
    store = pltpu.make_async_copy(short, sent, sems.at[2])
    store.start()

    def add(t, s1, s2):
        c1 = [coef[s1, b] for b in range(B)]
        c2 = [coef[s2, b] for b in range(B)]
        for r in range(8):
            rows = pl.ds(r * 16, 16)
            m1 = msg[s1, rows, :]
            m2 = msg[s2, rows, :]
            for b in range(B):
                sums[t, b, rows, :] = sums[t, b, rows, :] + (c1[b] * m1 + c2[b] * m2)

    pairs(order, filled, add)

    for t in range(TROWS):
        for b in range(B):
            part[pl.ds(t * TILE, TILE), pl.ds(b * H, H)] = sums[t, b].astype(BF16)
    outp[...] = jnp.dot(part[...], bases[...], preferred_element_type=F32).astype(BF16)
    mine = half[0]

    def outer(k):
        cols = pl.ds(pl.multiple_of(k * H, H), H)
        return lax.dot_general(
            part[:, cols], cot[...], (((0,), (0,)), ((), ())), preferred_element_type=F32
        )

    for k in range(B // 2):
        rows = pl.ds(k * H, H)
        dkeep[rows, :] = outer(mine * (B // 2) + k)
        dgive[rows, :] = outer((1 - mine) * (B // 2) + k).astype(BF16)
    store.wait()


def forward(trow, xslot, count, half, coef, xmine, xother, tiles, stacked, cot_rows):
    return pl.pallas_call(
        forward_kernel,
        in_specs=[SMEM] * 5 + [ANY] + [VMEM] * 4,
        out_specs=[VMEM] * 3 + [ANY],
        out_shape=[
            pltpu.VMEM((TROWS * TILE, H), BF16),
            pltpu.VMEM((1024, H), F32),
            pltpu.VMEM((1024, H), BF16),
            pltpu.HBM((SLOTS, TILE, H), BF16),
        ],
        scratch_shapes=[
            pltpu.VMEM((2 * SLOTS, TILE, H), BF16),
            pltpu.VMEM((TROWS, B, TILE, H), F32),
            pltpu.VMEM((TROWS * TILE, B * H), BF16),
            pltpu.VMEM((SLOTS + 1, TILE, H), F32),
            pltpu.VMEM((SLOTS, TILE, H), BF16),
            pltpu.SMEM((TROWS, SLOTS + 8), jnp.int32),
            pltpu.SMEM((TROWS,), jnp.int32),
            pltpu.SemaphoreType.DMA((3,)),
        ],
        compiler_params=PARAMS,
        name="forward",
    )(
        trow, xslot, count, half, coef,
        far(xmine), *map(near, (xother, tiles, stacked, cot_rows)),
    )


def gram_kernel(
    trow, count, relc, relr, sent, grads_in, coefg, msg, grads, gram, order, filled, sems
):
    loads = [
        pltpu.make_async_copy(sent, msg.at[pl.ds(0, SLOTS)], sems.at[0]),
        pltpu.make_async_copy(grads_in, grads, sems.at[1]),
    ]
    for copy in loads:
        copy.start()
    msg[SLOTS] = jnp.zeros((TILE, H), BF16)
    gram[...] = jnp.zeros_like(gram)
    by_row(trow, count, order, filled)
    for copy in loads:
        copy.wait()

    def dots(t, s1, s2):
        d1 = [jnp.zeros((8, 128), F32)] * B
        d2 = [jnp.zeros((8, 128), F32)] * B
        for r in range(8):
            rows = pl.ds(r * 16, 16)
            m1 = msg[s1, rows, :].astype(F32)
            m2 = msg[s2, rows, :].astype(F32)
            for b in range(B):
                g = grads[t, b, rows, :].astype(F32)
                d1[b] = d1[b] + fold(m1 * g)
                d2[b] = d2[b] + fold(m2 * g)
        for b in range(B):
            gram[s1, b] = d1[b]
            gram[s2, b] = d2[b]

    pairs(order, filled, dots)
    col = jnp.sum(jnp.sum(gram[pl.ds(0, SLOTS)].reshape(SLOTS * B, 8, 128), axis=1), axis=1, keepdims=True)
    lane = lax.broadcasted_iota(jnp.int32, (SLOTS * B, 128), 1)
    row = lax.broadcasted_iota(jnp.int32, (SLOTS * B, 128), 0)
    pick = (lane % B == row % B) & (lane // B == relc[...] % 16) & (row < count[0] * B)
    spread = jnp.where(pick, col, 0.0)
    line = lax.broadcasted_iota(jnp.int32, (32, SLOTS * B), 0)
    gather = (relr[...] // 16 == line).astype(F32)
    cg = jnp.dot(gather, spread, precision=lax.Precision.HIGHEST, preferred_element_type=F32)
    coefg[...] = cg


def gram_sums(trow, count, relc, relr, sent, grads):
    return pl.pallas_call(
        gram_kernel,
        in_specs=[SMEM] * 2 + [VMEM] * 2 + [ANY] * 2,
        out_specs=VMEM,
        out_shape=jax.ShapeDtypeStruct((32, 128), F32),
        scratch_shapes=[
            pltpu.VMEM((SLOTS + 1, TILE, H), BF16),
            pltpu.VMEM((TROWS, B, TILE, H), BF16),
            pltpu.VMEM((SLOTS + 1, B, 8, 128), F32),
            pltpu.SMEM((TROWS, SLOTS + 8), jnp.int32),
            pltpu.SMEM((TROWS,), jnp.int32),
            pltpu.SemaphoreType.DMA((2,)),
        ],
        compiler_params=PARAMS,
        name="gram",
    )(trow, count, relc, relr, far(sent), far(grads))


def swap(x):
    return lax.ppermute(x, "c", [(0, 1), (1, 0)])


def exchange(x, axes):
    return lax.all_to_all(x, axes, split_axis=0, concat_axis=0, tiled=True)


def spread_to(x, axes, n):
    return exchange(jnp.broadcast_to(x[None], (n,) + x.shape), axes)


def two_parts(x):
    hi = lax.reduce_precision(x, 8, 7)
    return jnp.concatenate([hi, x - hi], axis=-1).astype(BF16)


def one_part(x):
    return x[..., :128] + x[..., 128:]


def after(x, y):
    return lax.optimization_barrier((x, y))


def local(
    entity_feats,
    class_map,
    tile_values,
    tile_rows,
    tile_column_index,
    tile_rels,
    tile_counts,
    coefficients,
    bases,
    cotangent,
):
    mine = lax.axis_index("c").astype(jnp.int32)
    member = class_map[:, None] == jnp.arange(TILE, dtype=jnp.int32)[None, :]
    sums = lax.dot_general(
        member.astype(BF16), entity_feats, (((0,), (0,)), ((), ())), preferred_element_type=F32
    )
    counts = jnp.sum(member.astype(F32), axis=0)
    class_feat = (sums / counts[:, None]).astype(BF16)

    rels = jnp.pad(tile_rels, (0, 8), constant_values=-1)
    pick_rel = (rels[:, None] == jnp.arange(RELS, dtype=jnp.int32)[None, :]).astype(BF16)
    coef = jnp.dot(pick_rel, coefficients, preferred_element_type=F32)
    other = (tile_column_index % 2 != mine).astype(jnp.int32) * SLOTS
    ty = tile_column_index // (2 * NZ)
    tz = (tile_column_index // 2) % NZ
    xslot = other + tz * NY + ty
    dslot = other + ty * NZ + tz
    stacked = bases.reshape(B * H, H)

    with jax.named_scope("feats_y"):
        feats_y = spread_to(class_feat, "y", NY).reshape(NY * TILE, H)
    cotangent, feats_y = after(cotangent, feats_y)
    with jax.named_scope("feats_z"):
        feats_mine = lax.all_gather(feats_y, "z", axis=0, tiled=True)
    with jax.named_scope("cot_x"):
        cot_rows = lax.all_gather(cotangent, "x", axis=0, tiled=True)

    grads, keep, give = backward(
        tile_rows, dslot, tile_counts, coef, cot_rows, stacked, tile_values
    )
    with jax.named_scope("dx_c"):
        got = swap(give)
    dx = (keep.astype(F32) + got.astype(F32)).astype(BF16).reshape(NY * NZ * TILE, H)
    with jax.named_scope("dx_y"):
        dx = lax.psum_scatter(dx, "y", scatter_dimension=0, tiled=True)

    feats_mine = feats_mine.reshape(SLOTS, TILE, H)
    with jax.named_scope("feats_c"):
        feats_other = swap(feats_mine)
    rels = jnp.repeat(tile_rels, B)
    outp, dkeep, dgive, sent = forward(
        tile_rows, xslot, tile_counts, mine[None], coef,
        feats_mine, feats_other, tile_values, stacked, cot_rows,
    )

    with jax.named_scope("dv_c"):
        dgot = swap(dgive)
    dv = (dkeep + dgot.astype(F32)).reshape(NX, 256, H).astype(BF16)
    send_x = jnp.concatenate([dv, outp.reshape(NX, TILE, H)], axis=1)
    sent, dx = after(sent, dx.astype(F32))
    with jax.named_scope("dx_z"):
        dx = lax.psum_scatter(dx, "z", scatter_dimension=0, tiled=True)
    with jax.named_scope("dv_x"):
        got_x = exchange(send_x, "x")
    cg = gram_sums(tile_rows, tile_counts, rels[:, None], rels[None, :], sent, grads)
    (sum_x,) = lax.optimization_barrier((jnp.sum(got_x.astype(F32), axis=0),))
    layer_out = sum_x[256:].astype(BF16)
    pad = jnp.zeros((NY * NZ, 7, H), BF16)
    packed = jnp.concatenate(
        [sum_x[:256].reshape(NY * NZ, 8, H).astype(BF16), two_parts(cg)[:, None, :], pad], axis=1
    )
    with jax.named_scope("dv_yz"):
        got_yz = exchange(packed, ("y", "z"))
    sum_yz = jnp.sum(got_yz.astype(F32), axis=0)
    packed = jnp.concatenate(
        [sum_yz[:8].astype(BF16), two_parts(one_part(sum_yz[8:9])), jnp.zeros((7, H), BF16)], axis=0
    )
    with jax.named_scope("all_yz"):
        all_yz = spread_to(packed, ("y", "z"), NY * NZ)
    all_yz, dx = after(all_yz, dx)
    send_x = jnp.concatenate([all_yz[:, :8].reshape(256, H), all_yz[:, 8]], axis=0)
    with jax.named_scope("all_x"):
        all_x = spread_to(send_x, "x", NX)
    cg = two_parts(jnp.sum(one_part(all_x[:, 256:].astype(F32)), axis=0))
    send_c = jnp.concatenate([all_x[:, :256].reshape(1024, H), cg], axis=0)
    with jax.named_scope("all_c"):
        got_c = swap(send_c)
    scale = (NY * NZ * NC * NX * TILE) ** (-0.5)
    cg = one_part(send_c[1024:].astype(F32)) + one_part(got_c[1024:].astype(F32))
    grad_coef = (cg * scale).reshape(512, B)[:RELS]
    first = jnp.where(mine == 0, send_c[:1024], got_c[:1024])
    second = jnp.where(mine == 0, got_c[:1024], send_c[:1024])
    grad_bases = (jnp.stack([first, second]).astype(F32) * scale).reshape(B, H, H)

    quotient = dx / counts[:, None]
    grad_entities = jnp.dot(member.astype(F32), quotient, precision=lax.Precision.HIGHEST)
    return (layer_out, grad_entities, grad_bases, grad_coef)


def solution(mesh):
    grid = Mesh(mesh.devices.reshape(NY, NZ, NC, NX), DEVICES)
    by_tile = P(DEVICES)
    by_class = P(("x",) + ROWS)
    placed = (
        by_class,
        by_class,
        by_tile,
        by_tile,
        by_tile,
        by_tile,
        by_tile,
        P(),
        P(),
        by_tile,
    )
    return jax.shard_map(
        local,
        mesh=grid,
        in_specs=placed,
        out_specs=(by_tile, by_class, P(), P()),
        check_vma=False,
    )
```
